512 devices in a mesh: row: 32 (over x, y, core), col: 16 (over z).
Axes of the slice: x: 4, y: 4, z: 16, core: 2. Of those that a mesh axis runs over, the one named last changes fastest.
Arguments:
- tokens: bfloat16 [256, 8192], P('row', 'col'), may hold values from -6 to 6
- gate_weight: bfloat16 [8192, 24576], P('col', 'row'), may hold values from -0.0625 to 0.0625
- up_weight: bfloat16 [8192, 24576], P('col', 'row'), may hold values from -0.0625 to 0.0625
- down_weight: bfloat16 [24576, 8192], P('row', 'col'), may hold values from -0.0390625 to 0.0390625
- out_grad: bfloat16 [256, 8192], P('row', 'col'), may hold values from -1.5 to 1.5
Outputs:
- mixed: bfloat16 [256, 8192], P('row', 'col')
- input_grad: bfloat16 [256, 8192], P('row', 'col')
- gate_grad: bfloat16 [8192, 24576], P('col', 'row')
- up_grad: bfloat16 [8192, 24576], P('col', 'row')
- down_grad: bfloat16 [24576, 8192], P('row', 'col')
The draws below stay inside these ranges and needn't reach their ends.
All inputs are finite; a program needn't handle non-finite values.
Results may differ from the reference program's by a relative error of at most 0.0049.
Values may be sent and summed in bfloat16 or wider, within the bound.
A program may use at most 64 MiB of HBM per device.

```python
import jax
import jax.numpy as jnp
from jax import lax

D = 8192
FF = 24576
TOKENS = 256


def level_of(key, dims, pieces, least, high):
    loudness = 1.0
    for dim, blocks in pieces:
        draws = jax.random.uniform(jax.random.fold_in(jax.random.fold_in(key, 6), dim), (blocks,), jnp.float32, least / len(pieces), high / len(pieces))
        loudness = loudness * jnp.repeat(jnp.exp(draws), dims[dim] // blocks).reshape((-1,) + (1,) * (len(dims) - 1 - dim))
    return loudness


def noise(key, extent, spread, most, split=(), kind=jnp.bfloat16):
    factor_of = level_of(key, extent, split, -0.22, 0.18) if split else 1.0
    entries = jax.random.normal(key, extent, jnp.float32) * spread * factor_of
    return jnp.minimum(jnp.maximum(entries, -most), most).astype(kind)


def setup_inputs(seed: int = 0) -> dict:
    streams_of = jax.random.split(jax.random.key(seed), 6)
    tokens = noise(streams_of[0], (TOKENS, D), 1.0, 6.0, ((0, 32), (1, 16)))
    gate_weight = noise(streams_of[1], (D, FF), D ** -0.5, 0.0625, ((0, 16), (1, 32)))
    up_weight = noise(streams_of[2], (D, FF), D ** -0.5, 0.0625, ((0, 16), (1, 32)))
    down_weight = noise(streams_of[3], (FF, D), FF ** -0.5, 0.0390625, ((0, 32), (1, 16)))
    out_grad = noise(streams_of[4], (TOKENS, D), 0.25, 1.5, ((0, 32), (1, 16)))
    return dict(tokens=tokens, gate_weight=gate_weight, up_weight=up_weight, down_weight=down_weight, out_grad=out_grad)


def reference(tokens, gate_weight, up_weight, down_weight, out_grad):
    back = (((1,), (1,)), ((), ()))
    contract = (((0,), (0,)), ((), ()))
    gate = jnp.dot(tokens, gate_weight, preferred_element_type=jnp.float32)
    up = jnp.dot(tokens, up_weight, preferred_element_type=jnp.float32)
    hidden_grad = lax.dot_general(out_grad, down_weight, back, preferred_element_type=jnp.float32)
    sigmoid = jax.nn.sigmoid(gate)
    swish = gate * sigmoid
    hidden = (swish * up).astype(jnp.bfloat16)
    down_grad = lax.dot_general(hidden, out_grad, contract, preferred_element_type=jnp.float32).astype(jnp.bfloat16)
    gate_delta = (hidden_grad * up * sigmoid * (1.0 + gate * (1.0 - sigmoid))).astype(jnp.bfloat16)
    up_delta = (hidden_grad * swish).astype(jnp.bfloat16)
    gate_grad = lax.dot_general(tokens, gate_delta, contract, preferred_element_type=jnp.float32).astype(jnp.bfloat16)
    up_grad = lax.dot_general(tokens, up_delta, contract, preferred_element_type=jnp.float32).astype(jnp.bfloat16)
    mixed = jnp.dot(hidden, down_weight, preferred_element_type=jnp.float32)
    input_grad = lax.dot_general(gate_delta, gate_weight, back, preferred_element_type=jnp.float32)
    input_grad = input_grad + lax.dot_general(up_delta, up_weight, back, preferred_element_type=jnp.float32)
    return mixed.astype(jnp.bfloat16), input_grad.astype(jnp.bfloat16), gate_grad, up_grad, down_grad
```

```python
import functools

import jax
import jax.numpy as jnp
from jax import lax
from jax.experimental import pallas as pl
from jax.experimental.pallas import tpu as pltpu
from jax.sharding import PartitionSpec as P

MESH = pl.DeviceIdType.MESH
F32, BF16 = jnp.float32, jnp.bfloat16
NZ, NX, NY = 16, 4, 4
LANES, W = 3, 256

RIGHT = {1: 0, 2: 1, 3: 2, 4: 3, 5: 4, 6: 5, 7: 6, 8: 7}
LEFT = {-1: 0, -2: -1, -3: -2, -4: -3, -5: -4, -6: -5, -7: -6}
SUM_TREES = [{**RIGHT, **LEFT}] * LANES
SPREAD_TREES = [{**RIGHT, **LEFT}] * LANES


def mirrored(tree):
    return {-k: -p for k, p in tree.items()}


def children(tree, k):
    return [c for c, p in tree.items() if p == k]


def plan(sum_trees, spread_trees, sum_kb=48.0, spread_kb=24.0):
    free = {1: 0.0, -1: 0.0}
    arrive = {}
    clock = 0.0
    order = []

    def send(key, dist, kb, now):
        way = 1 if dist > 0 else -1
        hops = abs(dist)
        wire = kb * 2 * hops / 112.0
        begin = max(free[way], now)
        free[way] = begin + wire
        arrive[key] = begin + wire + 2.2 + 0.6 * hops

    todo = []
    for u in range(LANES):
        todo.append(("mm", u, 0))
        todo += [("sum", u, k) for k in sum_trees[u]]
        todo.append(("own", u, 0))
        todo += [("spread", u, k) for k in spread_trees[u] if children(spread_trees[u], k)]
        todo.append(("fin", u, 0))
        todo.append(("grad", u, 0))
    done = set()
    cost = {"mm": 0.8, "sum": 0.15, "own": 0.4, "spread": 0.08, "fin": 0.8, "grad": 0.9}
    last = {"mm": 0, "grad": 1e6}

    def ready(task):
        kind, u, k = task
        if kind == "mm":
            return 0.0 if u == 0 or ("mm", u - 1, 0) in done else None
        if kind == "sum" or kind == "own":
            if ("mm", u, 0) not in done:
                return None
            keys = [("sum", u, c) for c in children(sum_trees[u], k)]
        elif kind == "spread":
            keys = [("spread", u, k)]
        elif kind == "fin":
            if ("own", u, 0) not in done:
                return None
            keys = [("spread", u, c) for c in spread_trees[u]]
        else:
            return 0.0 if ("fin", u, 0) in done else None
        if any(key not in arrive for key in keys):
            return None
        return max([0.0] + [arrive[key] for key in keys])

    while todo:
        best = None
        for task in todo:
            at = ready(task)
            if at is None:
                continue
            rank = (max(at, clock) + last.get(task[0], 0.0) * 1.0, task[1], at)
            if best is None or rank < best[0]:
                best = (rank, task, at)
        _, task, at = best
        kind, u, k = task
        clock = max(clock, at) + cost[kind]
        if kind == "sum":
            send(("sum", u, k), k - sum_trees[u][k], sum_kb, clock)
        elif kind in ("own", "spread"):
            for c in children(spread_trees[u], k):
                send(("spread", u, c), c - k, spread_kb, clock)
        order.append(task)
        done.add(task)
        todo.remove(task)
    return order, clock


def offsets(sum_trees, spread_trees):
    found = set()
    for tree in sum_trees:
        found |= {(k - p) % NZ for k, p in tree.items()}
    for tree in spread_trees:
        found |= {(k - p) % NZ for k, p in tree.items()}
    found |= {(-o) % NZ for o in found}
    return sorted(found)


def torus(step):
    return min(step, 4 - step)


STEPS = sorted(
    [(dx, dy) for dx in range(NX) for dy in range(NY) if (dx, dy) != (0, 0)],
    key=lambda s: -(torus(s[0]) + torus(s[1])),
)
COLUMNS = [0, 1, 3, 2]


def dot(a, b, dims):
    return lax.dot_general(a, b, (dims, ((), ())), preferred_element_type=F32)


NN, NT, TN = ((1,), (0,)), ((1,), (1,)), ((0,), (0,))


def kernel(
    sum_trees, spread_trees, order,
    tok, gate_w, up_w, down_w, og,
    mixed, input_grad, gate_grad, up_grad, down_grad,
    gw, uw, dw, slabs, xs, gs, part, slot, acts, halves, sib, dsend, drecv, gg, ug, dg,
    w_sem, out_sem, a_send, a_recv, f_send, f_recv,
    sum_send, sum_recv, spread_send, spread_recv, h_send, h_recv, d_send, d_recv,
):
    row, z = lax.axis_index("row"), lax.axis_index("col")
    core, chip = row % 2, row // 2
    x, y = chip // NY, chip % NY
    sibling = (chip * 2 + 1 - core, z)

    loads = [
        pltpu.make_async_copy(src, dst, w_sem.at[i])
        for i, (src, dst) in enumerate(((gate_w, gw), (up_w, uw), (down_w, dw)))
    ]
    for load in loads:
        load.start()

    def plane(dx, dy):
        return ((x + dx) % NX) * NY + (y + dy) % NY

    barrier = pltpu.get_barrier_semaphore()
    around = offsets(sum_trees, spread_trees)
    for dx, dy in STEPS:
        pl.semaphore_signal(
            barrier, inc=1, device_id=(plane(dx, dy) * 2 + core, z), device_id_type=MESH
        )
    for o in around:
        pl.semaphore_signal(barrier, inc=1, device_id=(row, (z + o) % NZ), device_id_type=MESH)
    pl.semaphore_signal(barrier, inc=1, device_id=sibling, device_id_type=MESH)
    slabs[core, x, y] = jnp.concatenate(
        [tok[...].astype(F32), og[...].astype(F32)], axis=0
    ).astype(BF16)
    pl.semaphore_wait(barrier, len(STEPS) + len(around) + 1)

    def gather(dx, dy, from_x, from_y):
        return pltpu.make_async_remote_copy(
            src_ref=slabs.at[core, from_x, from_y],
            dst_ref=slabs.at[core, from_x, from_y],
            send_sem=a_send.at[dx * NY + dy],
            recv_sem=a_recv.at[dx * NY + dy],
            device_id=(plane(dx, dy) * 2 + core, z),
            device_id_type=MESH,
        )

    def forward(dx, which):
        return pltpu.make_async_remote_copy(
            src_ref=slabs.at[which, (x - dx) % NX],
            dst_ref=slabs.at[which, (x - dx) % NX],
            send_sem=f_send.at[dx],
            recv_sem=f_recv.at[dx],
            device_id=sibling,
            device_id_type=MESH,
        )

    for dx, dy in STEPS:
        gather(dx, dy, x, y).start()
    for dx in COLUMNS:
        for dy in range(NY):
            if (dx, dy) != (0, 0):
                gather(dx, dy, (x - dx) % NX, (y - dy) % NY).wait_recv()
        forward(dx, core).start()
    for load in loads:
        load.wait()
    for dx in COLUMNS:
        forward(dx, 1 - core).wait_recv()
    both = slabs[...].astype(F32)
    xs[...] = both[:, :, :, 0:8, :].reshape(256, 512).astype(BF16)
    gs[...] = both[:, :, :, 8:16, :].reshape(256, 512).astype(BF16)

    index = {k: i for i, k in enumerate(sorted(sum_trees[0]))}

    def sum_copy(u, k):
        o = k - sum_trees[u][k]
        return pltpu.make_async_remote_copy(
            src_ref=part.at[u, (z + k) % NZ],
            dst_ref=slot.at[u, index[k]],
            send_sem=sum_send.at[u, index[k]],
            recv_sem=sum_recv.at[u, index[k]],
            device_id=(row, (z + o) % NZ),
            device_id_type=MESH,
        )

    def spread_copy(u, c, chunk):
        o = c - spread_trees[u][c]
        return pltpu.make_async_remote_copy(
            src_ref=acts.at[u, chunk],
            dst_ref=acts.at[u, chunk],
            send_sem=spread_send.at[u, index[c]],
            recv_sem=spread_recv.at[u, index[c]],
            device_id=(row, (z + o) % NZ),
            device_id_type=MESH,
        )

    def spread_wait(u, k):
        spread_copy(u, k, (z - k) % NZ).wait_recv()

    for kind, u, k in order:
        unit = pl.ds(u * W, W)
        if kind == "mm":
            part[u, :, :, 0:W] = dot(xs[...], gw[:, unit], NN).reshape(NZ, 16, W)
            part[u, :, :, W : 2 * W] = dot(xs[...], uw[:, unit], NN).reshape(NZ, 16, W)
            part[u, :, :, 2 * W : 3 * W] = dot(gs[...], dw[unit, :], NT).reshape(NZ, 16, W)
        elif kind == "sum":
            below = children(sum_trees[u], k)
            if below:
                chunk = (z + k) % NZ
                total = part[u, chunk]
                for c in below:
                    sum_copy(u, c).wait_recv()
                    total += slot[u, index[c]]
                part[u, chunk] = total
            sum_copy(u, k).start()
        elif kind == "own":
            total = part[u, z]
            for c in children(sum_trees[u], 0):
                sum_copy(u, c).wait_recv()
                total += slot[u, index[c]]
            gate, up, hidden_grad = total[:, 0:W], total[:, W : 2 * W], total[:, 2 * W :]
            sig = jax.nn.sigmoid(gate)
            swish = gate * sig
            acts[u, z, :, 0:W] = (swish * up).astype(BF16)
            acts[u, z, :, W : 2 * W] = (
                hidden_grad * up * sig * (1.0 + gate * (1.0 - sig))
            ).astype(BF16)
            acts[u, z, :, 2 * W : 3 * W] = (hidden_grad * swish).astype(BF16)
            for c in children(spread_trees[u], 0):
                spread_copy(u, c, z).start()
        elif kind == "spread":
            spread_wait(u, k)
            for c in children(spread_trees[u], k):
                spread_copy(u, c, (z - k) % NZ).start()
        elif kind == "fin":
            for c in spread_trees[u]:
                if not children(spread_trees[u], c):
                    spread_wait(u, c)
            hidden = acts[u, :, :, 0:W].reshape(256, W)
            gate_delta = acts[u, :, :, W : 2 * W].reshape(256, W)
            up_delta = acts[u, :, :, 2 * W : 3 * W].reshape(256, W)
            out = dot(hidden, dw[unit, :], NN).reshape(2, 16, 8, 512)
            back = (dot(gate_delta, gw[:, unit], NT) + dot(up_delta, uw[:, unit], NT)).reshape(
                2, 16, 8, 512
            )
            if u != LANES_FIRST:
                out += halves[:, :, 0:8, :]
                back += halves[:, :, 8:16, :]
            halves[:, :, 0:8, :] = out
            halves[:, :, 8:16, :] = back
        else:
            hidden = acts[u, :, :, 0:W].reshape(256, W)
            gate_delta = acts[u, :, :, W : 2 * W].reshape(256, W)
            up_delta = acts[u, :, :, 2 * W : 3 * W].reshape(256, W)
            gg[:, unit] = dot(xs[...], gate_delta, TN).astype(BF16)
            ug[:, unit] = dot(xs[...], up_delta, TN).astype(BF16)
            dg[unit, :] = dot(hidden, gs[...], TN).astype(BF16)
        if kind == "fin" and (kind, u, k) == [t for t in order if t[0] == "fin"][-1]:
            half = pltpu.make_async_remote_copy(
                src_ref=halves.at[1 - core],
                dst_ref=sib,
                send_sem=h_send,
                recv_sem=h_recv,
                device_id=sibling,
                device_id_type=MESH,
            )
            half.start()
            half.wait_recv()

            def scatter(dx, dy):
                return pltpu.make_async_remote_copy(
                    src_ref=dsend.at[plane(dx, dy)],
                    dst_ref=drecv.at[dx * NY + dy],
                    send_sem=d_send.at[dx * NY + dy],
                    recv_sem=d_recv.at[dx * NY + dy],
                    device_id=(plane(dx, dy) * 2 + core, z),
                    device_id_type=MESH,
                )

            for dx, dy in STEPS:
                to = plane(dx, dy)
                dsend[to] = (halves[core, to] + sib[to]).astype(BF16)
                scatter(dx, dy).start()
            mine = halves[core, chip] + sib[chip]

    stores = [
        pltpu.make_async_copy(src, dst, out_sem.at[i])
        for i, (src, dst) in enumerate(((gg, gate_grad), (ug, up_grad), (dg, down_grad)))
    ]
    for store in stores:
        store.start()
    for dx, dy in reversed(STEPS):
        scatter(dx, dy).wait_recv()
        mine += drecv[dx * NY + dy].astype(F32)
    mixed[...] = mine[0:8].astype(BF16)
    input_grad[...] = mine[8:16].astype(BF16)
    for dx, dy in STEPS:
        gather(dx, dy, x, y).wait_send()
        scatter(dx, dy).wait_send()
    for dx in COLUMNS:
        forward(dx, core).wait_send()
    for u in range(LANES):
        for k in index:
            sum_copy(u, k).wait_send()
            spread_copy(u, k, z).wait_send()
    half.wait_send()
    for store in stores:
        store.wait()


LANES_FIRST = 0


def shards(tokens, gate_weight, up_weight, down_weight, out_grad):
    order, _ = plan(SUM_TREES, SPREAD_TREES)
    whole, anywhere = pl.BlockSpec(memory_space=pltpu.VMEM), pl.BlockSpec(memory_space=pl.ANY)
    dma = pltpu.SemaphoreType.DMA
    shape = jax.ShapeDtypeStruct
    outs = pl.pallas_call(
        functools.partial(kernel, SUM_TREES, SPREAD_TREES, order),
        out_shape=(
            shape((8, 512), BF16),
            shape((8, 512), BF16),
            shape((512, 768), BF16),
            shape((512, 768), BF16),
            shape((768, 512), BF16),
        ),
        in_specs=[whole, anywhere, anywhere, anywhere, whole],
        out_specs=(whole, whole, anywhere, anywhere, anywhere),
        scratch_shapes=[
            pltpu.VMEM((512, 768), BF16),
            pltpu.VMEM((512, 768), BF16),
            pltpu.VMEM((768, 512), BF16),
            pltpu.VMEM((2, NX, NY, 16, 512), BF16),
            pltpu.VMEM((256, 512), BF16),
            pltpu.VMEM((256, 512), BF16),
            pltpu.VMEM((LANES, NZ, 16, 3 * W), F32),
            pltpu.VMEM((LANES, NZ - 1, 16, 3 * W), F32),
            pltpu.VMEM((LANES, NZ, 16, 3 * W), BF16),
            pltpu.VMEM((2, 16, 16, 512), F32),
            pltpu.VMEM((16, 16, 512), F32),
            pltpu.VMEM((16, 16, 512), BF16),
            pltpu.VMEM((16, 16, 512), BF16),
            pltpu.VMEM((512, 768), BF16),
            pltpu.VMEM((512, 768), BF16),
            pltpu.VMEM((768, 512), BF16),
            dma((3,)), dma((3,)),
            dma((16,)), dma((16,)), dma((4,)), dma((4,)),
            dma((LANES, NZ - 1)), dma((LANES, NZ - 1)),
            dma((LANES, NZ - 1)), dma((LANES, NZ - 1)),
            dma, dma, dma((16,)), dma((16,)),
        ],
        compiler_params=pltpu.CompilerParams(
            collective_id=0, has_side_effects=True, vmem_limit_bytes=48 * 2**20
        ),
    )(tokens, gate_weight, up_weight, down_weight, out_grad)
    return outs


def solution(mesh):
    return jax.shard_map(
        shards,
        mesh=mesh,
        in_specs=(
            P("row", "col"),
            P("col", "row"),
            P("col", "row"),
            P("row", "col"),
            P("row", "col"),
        ),
        out_specs=(
            P("row", "col"),
            P("row", "col"),
            P("col", "row"),
            P("col", "row"),
            P("row", "col"),
        ),
        check_vma=False,
    )
```

```python
import functools

import jax
import jax.numpy as jnp
from jax import lax
from jax.experimental import pallas as pl
from jax.experimental.pallas import tpu as pltpu
from jax.sharding import PartitionSpec as P

MESH = pl.DeviceIdType.MESH
F32, BF16 = jnp.float32, jnp.bfloat16
NZ, NX, NY = 16, 4, 4
LANES, W = 3, 256

SUM_FAR = {1: 0, 2: 1, 3: 2, 4: 3, 5: 6, 6: 2, 7: 6, 8: 6}
SUM_NEAR = {1: 0, 2: 1, 3: 2, 4: 5, 5: 1, 6: 5, 7: 5}
WIDE_FAR, WIDE_NEAR = (1, 2), (1,)
SPREAD_FAR = {1: 0, 2: 1, 3: 4, 4: 0, 5: 4, 6: 4, 7: 6, 8: 6}
SPREAD_NEAR = {1: 0, 2: 1, 3: 4, 4: 0, 5: 4, 6: 4, 7: 6}
RATE, FIXED, HOP = 85.0, 2.35, 0.65


def two_sided(far, near, way):
    return {**{way * k: way * p for k, p in far.items()}, **{-way * k: -way * p for k, p in near.items()}}


def sides(u):
    return 1 if u % 2 == 0 else -1


def trees():
    sums = [two_sided(SUM_FAR, SUM_NEAR, sides(u)) for u in range(LANES)]
    wide = [
        {sides(u) * k for k in WIDE_FAR} | {-sides(u) * k for k in WIDE_NEAR} for u in range(LANES)
    ]
    spreads = [two_sided(SPREAD_FAR, SPREAD_NEAR, -sides(u)) for u in range(LANES)]
    return sums, wide, spreads


def children(tree, k):
    return [c for c, p in tree.items() if p == k]


def plan(sum_trees, wide, spread_trees):
    kb = 72.0 / LANES
    free = {1: 0.0, -1: 0.0}
    arrive = {}
    clock = 0.0
    order = []

    def send(key, dist, kb, now):
        way = 1 if dist > 0 else -1
        hops = abs(dist)
        wire = kb * 2 * hops / RATE
        begin = max(free[way], now)
        free[way] = begin + wire
        arrive[key] = begin + wire + FIXED + HOP * hops

    todo = []
    for u in range(LANES):
        todo.append(("mm", u, 0))
        todo += [("sum", u, k) for k in sum_trees[u]]
        todo.append(("own", u, 0))
        todo += [("spread", u, k) for k in spread_trees[u] if children(spread_trees[u], k)]
        todo.append(("fin", u, 0))
        todo.append(("grad", u, 0))
    done = set()
    cost = {"mm": 0.33, "sum": 0.06, "own": 0.1, "spread": 0.04, "fin": 0.3, "grad": 0.17}
    last = {"mm": 0, "grad": 1e6}

    def ready(task):
        kind, u, k = task
        if kind == "mm":
            return 0.0 if u == 0 or ("mm", u - 1, 0) in done else None
        if kind == "sum" or kind == "own":
            if ("mm", u, 0) not in done:
                return None
            keys = [("sum", u, c) for c in children(sum_trees[u], k)]
        elif kind == "spread":
            keys = [("spread", u, k)]
        elif kind == "fin":
            if ("own", u, 0) not in done:
                return None
            keys = [("spread", u, c) for c in spread_trees[u]]
        else:
            return 0.0 if ("fin", u, 0) in done else None
        if any(key not in arrive for key in keys):
            return None
        return max([0.0] + [arrive[key] for key in keys])

    while todo:
        best = None
        for task in todo:
            at = ready(task)
            if at is None:
                continue
            rank = (max(at, clock) + last.get(task[0], 0.0), task[1], at)
            if best is None or rank < best[0]:
                best = (rank, task, at)
        _, task, at = best
        kind, u, k = task
        clock = max(clock, at) + cost[kind]
        if kind == "sum":
            send(("sum", u, k), k - sum_trees[u][k], kb * (2 if k in wide[u] else 1), clock)
        elif kind in ("own", "spread"):
            for c in children(spread_trees[u], k):
                send(("spread", u, c), c - k, kb, clock)
        order.append(task)
        done.add(task)
        todo.remove(task)
    return order, clock


def offsets(sum_trees, spread_trees):
    found = set()
    for tree in sum_trees:
        found |= {(k - p) % NZ for k, p in tree.items()}
    for tree in spread_trees:
        found |= {(k - p) % NZ for k, p in tree.items()}
    found |= {(-o) % NZ for o in found}
    return sorted(found)


def torus(step):
    return min(step, 4 - step)


STEPS = sorted(
    [(dx, dy) for dx in range(NX) for dy in range(NY) if (dx, dy) != (0, 0)],
    key=lambda s: -(torus(s[0]) + torus(s[1])),
)
COLUMNS = [0, 1, 3, 2]


def dot(a, b, dims):
    return lax.dot_general(a, b, (dims, ((), ())), preferred_element_type=F32)


NN, NT, TN = ((1,), (0,)), ((1,), (1,)), ((0,), (0,))


def kernel(
    sum_trees, wide, spread_trees, order,
    tok, gate_w, up_w, down_w, og,
    mixed, input_grad, gate_grad, up_grad, down_grad,
    gw, uw, dw, slabs, xs, gs, part, slot, low_out, low_in, acts, halves, sib, dsend, drecv, gg, ug, dg,
    w_sem, out_sem, a_send, a_recv, f_send, f_recv,
    sum_send, sum_recv, spread_send, spread_recv, h_send, h_recv, d_send, d_recv,
):
    row, z = lax.axis_index("row"), lax.axis_index("col")
    core, chip = row % 2, row // 2
    x, y = chip // NY, chip % NY
    sibling = (chip * 2 + 1 - core, z)

    loads = [
        pltpu.make_async_copy(src, dst, w_sem.at[i])
        for i, (src, dst) in enumerate(((gate_w, gw), (up_w, uw), (down_w, dw)))
    ]
    for load in loads:
        load.start()

    def plane(dx, dy):
        return ((x + dx) % NX) * NY + (y + dy) % NY

    barrier = pltpu.get_barrier_semaphore()
    around = offsets(sum_trees, spread_trees)
    for dx, dy in STEPS:
        pl.semaphore_signal(
            barrier, inc=1, device_id=(plane(dx, dy) * 2 + core, z), device_id_type=MESH
        )
    for o in around:
        pl.semaphore_signal(barrier, inc=1, device_id=(row, (z + o) % NZ), device_id_type=MESH)
    pl.semaphore_signal(barrier, inc=1, device_id=sibling, device_id_type=MESH)
    slabs[core, x, y] = jnp.concatenate(
        [tok[...].astype(F32), og[...].astype(F32)], axis=0
    ).astype(BF16)
    pl.semaphore_wait(barrier, len(STEPS) + len(around) + 1)

    def gather(dx, dy, from_x, from_y):
        return pltpu.make_async_remote_copy(
            src_ref=slabs.at[core, from_x, from_y],
            dst_ref=slabs.at[core, from_x, from_y],
            send_sem=a_send.at[dx * NY + dy],
            recv_sem=a_recv.at[dx * NY + dy],
            device_id=(plane(dx, dy) * 2 + core, z),
            device_id_type=MESH,
        )

    def forward(dx, which):
        return pltpu.make_async_remote_copy(
            src_ref=slabs.at[which, (x - dx) % NX],
            dst_ref=slabs.at[which, (x - dx) % NX],
            send_sem=f_send.at[dx],
            recv_sem=f_recv.at[dx],
            device_id=sibling,
            device_id_type=MESH,
        )

    for dx, dy in STEPS:
        gather(dx, dy, x, y).start()
    for dx in COLUMNS:
        for dy in range(NY):
            if (dx, dy) in STEPS:
                gather(dx, dy, (x - dx) % NX, (y - dy) % NY).wait_recv()
        forward(dx, core).start()
    for load in loads:
        load.wait()
    for dx in COLUMNS:
        forward(dx, 1 - core).wait_recv()
    both = slabs[...].astype(F32)
    xs[...] = both[:, :, :, 0:8, :].reshape(256, 512).astype(BF16)
    gs[...] = both[:, :, :, 8:16, :].reshape(256, 512).astype(BF16)

    def index(tree, k):
        return sorted(tree).index(k)

    def sum_copy(u, k):
        o = k - sum_trees[u][k]
        i = index(sum_trees[u], k)
        return pltpu.make_async_remote_copy(
            src_ref=part.at[u, (z + k) % NZ] if k in wide[u] else low_out.at[u, i],
            dst_ref=slot.at[u, i] if k in wide[u] else low_in.at[u, i],
            send_sem=sum_send.at[u, i],
            recv_sem=sum_recv.at[u, i],
            device_id=(row, (z + o) % NZ),
            device_id_type=MESH,
        )

    def spread_copy(u, c, chunk):
        o = c - spread_trees[u][c]
        i = index(spread_trees[u], c)
        return pltpu.make_async_remote_copy(
            src_ref=acts.at[u, chunk],
            dst_ref=acts.at[u, chunk],
            send_sem=spread_send.at[u, i],
            recv_sem=spread_recv.at[u, i],
            device_id=(row, (z + o) % NZ),
            device_id_type=MESH,
        )

    def gathered(u, k, total):
        for c in children(sum_trees[u], k):
            sum_copy(u, c).wait_recv()
            i = index(sum_trees[u], c)
            total += slot[u, i] if c in wide[u] else low_in[u, i].astype(F32)
        return total

    def spread_wait(u, k):
        spread_copy(u, k, (z - k) % NZ).wait_recv()

    for kind, u, k in order:
        unit = pl.ds(u * W, W)
        if kind == "mm":
            part[u, :, :, 0:W] = dot(xs[...], gw[:, unit], NN).reshape(NZ, 16, W)
            part[u, :, :, W : 2 * W] = dot(xs[...], uw[:, unit], NN).reshape(NZ, 16, W)
            part[u, :, :, 2 * W : 3 * W] = dot(gs[...], dw[unit, :], NT).reshape(NZ, 16, W)
        elif kind == "sum":
            chunk = (z + k) % NZ
            total = gathered(u, k, part[u, chunk])
            if k not in wide[u]:
                low_out[u, index(sum_trees[u], k)] = total.astype(BF16)
            elif children(sum_trees[u], k):
                part[u, chunk] = total
            sum_copy(u, k).start()
        elif kind == "own":
            total = gathered(u, 0, part[u, z])
            gate, up, hidden_grad = total[:, 0:W], total[:, W : 2 * W], total[:, 2 * W :]
            sig = jax.nn.sigmoid(gate)
            swish = gate * sig
            acts[u, z, :, 0:W] = (swish * up).astype(BF16)
            acts[u, z, :, W : 2 * W] = (
                hidden_grad * up * sig * (1.0 + gate * (1.0 - sig))
            ).astype(BF16)
            acts[u, z, :, 2 * W : 3 * W] = (hidden_grad * swish).astype(BF16)
            for c in children(spread_trees[u], 0):
                spread_copy(u, c, z).start()
        elif kind == "spread":
            spread_wait(u, k)
            for c in children(spread_trees[u], k):
                spread_copy(u, c, (z - k) % NZ).start()
        elif kind == "fin":
            for c in spread_trees[u]:
                if not children(spread_trees[u], c):
                    spread_wait(u, c)
            hidden = acts[u, :, :, 0:W].reshape(256, W)
            gate_delta = acts[u, :, :, W : 2 * W].reshape(256, W)
            up_delta = acts[u, :, :, 2 * W : 3 * W].reshape(256, W)
            out = dot(hidden, dw[unit, :], NN).reshape(2, 16, 8, 512)
            back = (dot(gate_delta, gw[:, unit], NT) + dot(up_delta, uw[:, unit], NT)).reshape(
                2, 16, 8, 512
            )
            if u != LANES_FIRST:
                out += halves[:, :, 0:8, :]
                back += halves[:, :, 8:16, :]
            halves[:, :, 0:8, :] = out
            halves[:, :, 8:16, :] = back
        else:
            hidden = acts[u, :, :, 0:W].reshape(256, W)
            gate_delta = acts[u, :, :, W : 2 * W].reshape(256, W)
            up_delta = acts[u, :, :, 2 * W : 3 * W].reshape(256, W)
            gg[:, unit] = dot(xs[...], gate_delta, TN).astype(BF16)
            ug[:, unit] = dot(xs[...], up_delta, TN).astype(BF16)
            dg[unit, :] = dot(hidden, gs[...], TN).astype(BF16)
        if kind == "fin" and (kind, u, k) == [t for t in order if t[0] == "fin"][-1]:
            half = pltpu.make_async_remote_copy(
                src_ref=halves.at[1 - core],
                dst_ref=sib,
                send_sem=h_send,
                recv_sem=h_recv,
                device_id=sibling,
                device_id_type=MESH,
            )
            half.start()
            half.wait_recv()

            def scatter(dx, dy):
                return pltpu.make_async_remote_copy(
                    src_ref=dsend.at[plane(dx, dy)],
                    dst_ref=drecv.at[dx * NY + dy],
                    send_sem=d_send.at[dx * NY + dy],
                    recv_sem=d_recv.at[dx * NY + dy],
                    device_id=(plane(dx, dy) * 2 + core, z),
                    device_id_type=MESH,
                )

            for dx, dy in STEPS:
                to = plane(dx, dy)
                dsend[to] = (halves[core, to] + sib[to]).astype(BF16)
                scatter(dx, dy).start()
            mine = halves[core, chip] + sib[chip]

    stores = [
        pltpu.make_async_copy(src, dst, out_sem.at[i])
        for i, (src, dst) in enumerate(((gg, gate_grad), (ug, up_grad), (dg, down_grad)))
    ]
    for store in stores:
        store.start()
    for dx, dy in reversed(STEPS):
        scatter(dx, dy).wait_recv()
        mine += drecv[dx * NY + dy].astype(F32)
    mixed[...] = mine[0:8].astype(BF16)
    input_grad[...] = mine[8:16].astype(BF16)
    for dx, dy in STEPS:
        gather(dx, dy, x, y).wait_send()
        scatter(dx, dy).wait_send()
    for dx in COLUMNS:
        forward(dx, core).wait_send()
    for u in range(LANES):
        for k in sum_trees[u]:
            sum_copy(u, k).wait_send()
        for k in spread_trees[u]:
            spread_copy(u, k, z).wait_send()
    half.wait_send()
    for store in stores:
        store.wait()


LANES_FIRST = 0


def hand_on(pieces, *refs):
    sources, targets, held, (in_sem, out_sem) = refs[:5], refs[5:10], refs[10:15], refs[15:]

    def rows(ref, j, n):
        return ref if n == ref.shape[0] else ref.at[pl.ds(j * n, n)]

    loads = [
        pltpu.make_async_copy(rows(sources[i], j, n), rows(held[i], j, n), in_sem.at[p])
        for p, (i, j, n) in enumerate(pieces)
    ]
    stores = [
        pltpu.make_async_copy(rows(held[i], j, n), rows(targets[i], j, n), out_sem.at[p])
        for p, (i, j, n) in enumerate(pieces)
    ]
    for load in loads:
        load.start()
    for load, store in zip(loads, stores):
        load.wait()
        store.start()
    for store in stores:
        store.wait()


def shards(tokens, gate_weight, up_weight, down_weight, out_grad):
    sum_trees, wide, spread_trees = trees()
    order, _ = plan(sum_trees, wide, spread_trees)
    whole, anywhere = pl.BlockSpec(memory_space=pltpu.VMEM), pl.BlockSpec(memory_space=pl.ANY)
    dma = pltpu.SemaphoreType.DMA
    shape = jax.ShapeDtypeStruct
    outs = pl.pallas_call(
        functools.partial(kernel, sum_trees, wide, spread_trees, order),
        out_shape=(
            shape((8, 512), BF16),
            shape((8, 512), BF16),
            shape((512, 768), BF16),
            shape((512, 768), BF16),
            shape((768, 512), BF16),
        ),
        in_specs=[whole, anywhere, anywhere, anywhere, whole],
        out_specs=(whole, whole, anywhere, anywhere, anywhere),
        scratch_shapes=[
            pltpu.VMEM((512, 768), BF16),
            pltpu.VMEM((512, 768), BF16),
            pltpu.VMEM((768, 512), BF16),
            pltpu.VMEM((2, NX, NY, 16, 512), BF16),
            pltpu.VMEM((256, 512), BF16),
            pltpu.VMEM((256, 512), BF16),
            pltpu.VMEM((LANES, NZ, 16, 3 * W), F32),
            pltpu.VMEM((LANES, NZ - 1, 16, 3 * W), F32),
            pltpu.VMEM((LANES, NZ - 1, 16, 3 * W), BF16),
            pltpu.VMEM((LANES, NZ - 1, 16, 3 * W), BF16),
            pltpu.VMEM((LANES, NZ, 16, 3 * W), BF16),
            pltpu.VMEM((2, 16, 16, 512), F32),
            pltpu.VMEM((16, 16, 512), F32),
            pltpu.VMEM((16, 16, 512), BF16),
            pltpu.VMEM((16, 16, 512), BF16),
            pltpu.VMEM((512, 768), BF16),
            pltpu.VMEM((512, 768), BF16),
            pltpu.VMEM((768, 512), BF16),
            dma((3,)), dma((3,)),
            dma((16,)), dma((16,)), dma((4,)), dma((4,)),
            dma((LANES, NZ - 1)), dma((LANES, NZ - 1)),
            dma((LANES, NZ - 1)), dma((LANES, NZ - 1)),
            dma, dma, dma((16,)), dma((16,)),
        ],
        compiler_params=pltpu.CompilerParams(
            collective_id=0, has_side_effects=True, vmem_limit_bytes=62 * 2**20
        ),
    )(tokens, gate_weight, up_weight, down_weight, out_grad)
    pieces = [(i, 0, o.shape[0]) for i, o in enumerate(outs[:2])]
    pieces += [(i, j, o.shape[0] // 4) for i, o in enumerate(outs) if i > 1 for j in range(4)]
    return pl.pallas_call(
        functools.partial(hand_on, pieces),
        out_shape=tuple(shape(o.shape, o.dtype) for o in outs),
        in_specs=[anywhere] * 5,
        out_specs=(anywhere,) * 5,
        scratch_shapes=[pltpu.VMEM(o.shape, o.dtype) for o in outs]
        + [dma((len(pieces),)), dma((len(pieces),))],
    )(*outs)


def solution(mesh):
    return jax.shard_map(
        shards,
        mesh=mesh,
        in_specs=(
            P("row", "col"),
            P("col", "row"),
            P("col", "row"),
            P("row", "col"),
            P("row", "col"),
        ),
        out_specs=(
            P("row", "col"),
            P("row", "col"),
            P("col", "row"),
            P("col", "row"),
            P("row", "col"),
        ),
        check_vma=False,
    )
```

```python
import functools

import jax
import jax.numpy as jnp
from jax import lax
from jax.experimental import pallas as pl
from jax.experimental.pallas import tpu as pltpu
from jax.sharding import PartitionSpec as P

MESH = pl.DeviceIdType.MESH
F32, BF16 = jnp.float32, jnp.bfloat16
NZ, NX, NY = 16, 4, 4
LANES, W = 3, 256

SUM_FAR = {1: 0, 2: 1, 3: 2, 4: 3, 5: 6, 6: 3, 7: 6, 8: 6}
SUM_NEAR = {1: 0, 2: 1, 3: 2, 4: 5, 5: 2, 6: 5, 7: 5}
WIDE_FAR, WIDE_NEAR = (1, 2, 3), (1, 2)
SPREAD_FAR = {1: 0, 2: 3, 3: 0, 4: 3, 5: 6, 6: 3, 7: 6, 8: 6}
SPREAD_NEAR = {1: 0, 2: 3, 3: 0, 4: 3, 5: 3, 6: 5, 7: 5}
RATE, BURST, FIXED, HOP = 95.0, 130.0, 2.35, 0.65


def two_sided(far, near, way):
    return {**{way * k: way * p for k, p in far.items()}, **{-way * k: -way * p for k, p in near.items()}}


def sides(u):
    return 1 if u % 2 == 0 else -1


def trees():
    sums = [two_sided(SUM_FAR, SUM_NEAR, sides(u)) for u in range(LANES)]
    wide = [
        {sides(u) * k for k in WIDE_FAR} | {-sides(u) * k for k in WIDE_NEAR} for u in range(LANES)
    ]
    spreads = [two_sided(SPREAD_FAR, SPREAD_NEAR, -sides(u)) for u in range(LANES)]
    return sums, wide, spreads


def children(tree, k):
    return sorted((c for c, p in tree.items() if p == k), key=lambda c: -abs(c - k))


def plan(sum_trees, wide, spread_trees):
    kb = 72.0 / LANES
    free = {1: 0.0, -1: 0.0}
    arrive = {}
    clock = 0.0
    order = []

    def send(key, dist, kb, now):
        way = 1 if dist > 0 else -1
        hops = abs(dist)
        begin = max(free[way], now)
        free[way] = begin + kb * 2 * hops / RATE
        arrive[key] = begin + kb * 2 / BURST + FIXED + HOP * hops

    todo = []
    for u in range(LANES):
        todo.append(("mm", u, 0))
        todo += [("sum", u, k) for k in sorted(sum_trees[u], key=lambda k: -abs(k - sum_trees[u][k]))]
        todo.append(("own", u, 0))
        todo += [("spread", u, k) for k in spread_trees[u] if children(spread_trees[u], k)]
        todo.append(("fin", u, 0))
        todo.append(("grad", u, 0))
    done = set()
    cost = {"mm": 0.33, "sum": 0.06, "own": 0.1, "spread": 0.04, "fin": 0.3, "grad": 0.17}
    last = {"mm": 0, "grad": 1e6}

    def ready(task):
        kind, u, k = task
        if kind == "mm":
            return 0.0 if u == 0 or ("mm", u - 1, 0) in done else None
        if kind == "sum" or kind == "own":
            if ("mm", u, 0) not in done:
                return None
            keys = [("sum", u, c) for c in children(sum_trees[u], k)]
        elif kind == "spread":
            keys = [("spread", u, k)]
        elif kind == "fin":
            if ("own", u, 0) not in done:
                return None
            keys = [("spread", u, c) for c in spread_trees[u]]
        else:
            return 0.0 if ("fin", u, 0) in done else None
        if any(key not in arrive for key in keys):
            return None
        return max([0.0] + [arrive[key] for key in keys])

    while todo:
        best = None
        for task in todo:
            at = ready(task)
            if at is None:
                continue
            rank = (max(at, clock) + last.get(task[0], 0.0), task[1], at)
            if best is None or rank < best[0]:
                best = (rank, task, at)
        _, task, at = best
        kind, u, k = task
        clock = max(clock, at) + cost[kind]
        if kind == "sum":
            send(("sum", u, k), k - sum_trees[u][k], kb * (2 if k in wide[u] else 1), clock)
        elif kind in ("own", "spread"):
            for c in children(spread_trees[u], k):
                send(("spread", u, c), c - k, kb, clock)
        order.append(task)
        done.add(task)
        todo.remove(task)
    return order, clock


def offsets(sum_trees, spread_trees):
    found = set()
    for tree in sum_trees:
        found |= {(k - p) % NZ for k, p in tree.items()}
    for tree in spread_trees:
        found |= {(k - p) % NZ for k, p in tree.items()}
    found |= {(-o) % NZ for o in found}
    return sorted(found)


def torus(step):
    return min(step, 4 - step)


STEPS = sorted(
    [(dx, dy) for dx in range(NX) for dy in range(NY) if (dx, dy) != (0, 0)],
    key=lambda s: -(torus(s[0]) + torus(s[1])),
)
COLUMNS = [0, 1, 3, 2]


def dot(a, b, dims):
    return lax.dot_general(a, b, (dims, ((), ())), preferred_element_type=F32)


NN, NT, TN = ((1,), (0,)), ((1,), (1,)), ((0,), (0,))


def kernel(
    sum_trees, wide, spread_trees, order,
    tok, gate_w, up_w, down_w, og,
    mixed, input_grad, gate_grad, up_grad, down_grad,
    own, mine, gw, uw, dw, slabs, xs, gs, part, slot, low_out, low_in, acts, halves, sib, dsend, drecv, gg, ug, dg,
    w_sem, out_sem, a_send, a_recv, f_send, f_recv,
    sum_send, sum_recv, spread_send, spread_recv, h_send, h_recv, d_send, d_recv,
):
    row, z = lax.axis_index("row"), lax.axis_index("col")
    core, chip = row % 2, row // 2
    x, y = chip // NY, chip % NY
    sibling = (chip * 2 + 1 - core, z)

    def plane(dx, dy):
        return ((x + dx) % NX) * NY + (y + dy) % NY

    barrier = pltpu.get_barrier_semaphore()
    around = offsets(sum_trees, spread_trees)
    for dx, dy in STEPS:
        pl.semaphore_signal(
            barrier, inc=1, device_id=(plane(dx, dy) * 2 + core, z), device_id_type=MESH
        )
    for o in around:
        pl.semaphore_signal(barrier, inc=1, device_id=(row, (z + o) % NZ), device_id_type=MESH)
    pl.semaphore_signal(barrier, inc=1, device_id=sibling, device_id_type=MESH)
    loads = [
        pltpu.make_async_copy(src, dst, w_sem.at[i])
        for i, (src, dst) in enumerate(
            ((gate_w, gw), (up_w, uw), (down_w, dw), (tok, own.at[0]), (og, own.at[1]))
        )
    ]
    for load in reversed(loads):
        load.start()
    for load in loads[3:]:
        load.wait()
    slabs[core, x, y] = jnp.concatenate([own[0].astype(F32), own[1].astype(F32)], axis=0).astype(BF16)
    pl.semaphore_wait(barrier, len(STEPS) + len(around) + 1)

    def gather(dx, dy, from_x, from_y):
        return pltpu.make_async_remote_copy(
            src_ref=slabs.at[core, from_x, from_y],
            dst_ref=slabs.at[core, from_x, from_y],
            send_sem=a_send.at[dx * NY + dy],
            recv_sem=a_recv.at[dx * NY + dy],
            device_id=(plane(dx, dy) * 2 + core, z),
            device_id_type=MESH,
        )

    def forward(dx, which):
        return pltpu.make_async_remote_copy(
            src_ref=slabs.at[which, (x - dx) % NX],
            dst_ref=slabs.at[which, (x - dx) % NX],
            send_sem=f_send.at[dx],
            recv_sem=f_recv.at[dx],
            device_id=sibling,
            device_id_type=MESH,
        )

    for dx, dy in STEPS:
        gather(dx, dy, x, y).start()
    for dx in COLUMNS:
        for dy in range(NY):
            if (dx, dy) in STEPS:
                gather(dx, dy, (x - dx) % NX, (y - dy) % NY).wait_recv()
        forward(dx, core).start()
    for load in loads[:3]:
        load.wait()
    for dx in COLUMNS:
        forward(dx, 1 - core).wait_recv()
    both = slabs[...].astype(F32)
    xs[...] = both[:, :, :, 0:8, :].reshape(256, 512).astype(BF16)
    gs[...] = both[:, :, :, 8:16, :].reshape(256, 512).astype(BF16)

    def index(tree, k):
        return sorted(tree).index(k)

    def sum_copy(u, k):
        o = k - sum_trees[u][k]
        i = index(sum_trees[u], k)
        return pltpu.make_async_remote_copy(
            src_ref=part.at[u, (z + k) % NZ] if k in wide[u] else low_out.at[u, i],
            dst_ref=slot.at[u, i] if k in wide[u] else low_in.at[u, i],
            send_sem=sum_send.at[u, i],
            recv_sem=sum_recv.at[u, i],
            device_id=(row, (z + o) % NZ),
            device_id_type=MESH,
        )

    def spread_copy(u, c, chunk):
        o = c - spread_trees[u][c]
        i = index(spread_trees[u], c)
        return pltpu.make_async_remote_copy(
            src_ref=acts.at[u, chunk],
            dst_ref=acts.at[u, chunk],
            send_sem=spread_send.at[u, i],
            recv_sem=spread_recv.at[u, i],
            device_id=(row, (z + o) % NZ),
            device_id_type=MESH,
        )

    def gathered(u, k, total):
        for c in children(sum_trees[u], k):
            sum_copy(u, c).wait_recv()
            i = index(sum_trees[u], c)
            total += slot[u, i] if c in wide[u] else low_in[u, i].astype(F32)
        return total

    def spread_wait(u, k):
        spread_copy(u, k, (z - k) % NZ).wait_recv()

    begun = False
    for kind, u, k in order:
        unit = pl.ds(u * W, W)
        if kind == "mm":
            part[u, :, :, 0:W] = dot(xs[...], gw[:, unit], NN).reshape(NZ, 16, W)
            part[u, :, :, W : 2 * W] = dot(xs[...], uw[:, unit], NN).reshape(NZ, 16, W)
            part[u, :, :, 2 * W : 3 * W] = dot(gs[...], dw[unit, :], NT).reshape(NZ, 16, W)
        elif kind == "sum":
            chunk = (z + k) % NZ
            total = gathered(u, k, part[u, chunk])
            if k not in wide[u]:
                low_out[u, index(sum_trees[u], k)] = total.astype(BF16)
            elif children(sum_trees[u], k):
                part[u, chunk] = total
            sum_copy(u, k).start()
        elif kind == "own":
            total = gathered(u, 0, part[u, z])
            gate, up, hidden_grad = total[:, 0:W], total[:, W : 2 * W], total[:, 2 * W :]
            sig = jax.nn.sigmoid(gate)
            swish = gate * sig
            acts[u, z, :, 0:W] = (swish * up).astype(BF16)
            acts[u, z, :, W : 2 * W] = (
                hidden_grad * up * sig * (1.0 + gate * (1.0 - sig))
            ).astype(BF16)
            acts[u, z, :, 2 * W : 3 * W] = (hidden_grad * swish).astype(BF16)
            for c in children(spread_trees[u], 0):
                spread_copy(u, c, z).start()
        elif kind == "spread":
            spread_wait(u, k)
            for c in children(spread_trees[u], k):
                spread_copy(u, c, (z - k) % NZ).start()
        elif kind == "fin":
            for c in spread_trees[u]:
                if not children(spread_trees[u], c):
                    spread_wait(u, c)
            hidden = acts[u, :, :, 0:W].reshape(256, W)
            gate_delta = acts[u, :, :, W : 2 * W].reshape(256, W)
            up_delta = acts[u, :, :, 2 * W : 3 * W].reshape(256, W)
            out = dot(hidden, dw[unit, :], NN).reshape(2, 16, 8, 512)
            back = (dot(gate_delta, gw[:, unit], NT) + dot(up_delta, uw[:, unit], NT)).reshape(
                2, 16, 8, 512
            )
            if begun:
                out += halves[:, :, 0:8, :]
                back += halves[:, :, 8:16, :]
            halves[:, :, 0:8, :] = out
            halves[:, :, 8:16, :] = back
            begun = True
        else:
            hidden = acts[u, :, :, 0:W].reshape(256, W)
            gate_delta = acts[u, :, :, W : 2 * W].reshape(256, W)
            up_delta = acts[u, :, :, 2 * W : 3 * W].reshape(256, W)
            gg[:, unit] = dot(xs[...], gate_delta, TN).astype(BF16)
            ug[:, unit] = dot(xs[...], up_delta, TN).astype(BF16)
            dg[unit, :] = dot(hidden, gs[...], TN).astype(BF16)
        if kind == "fin" and (kind, u, k) == [t for t in order if t[0] == "fin"][-1]:
            half = pltpu.make_async_remote_copy(
                src_ref=halves.at[1 - core],
                dst_ref=sib,
                send_sem=h_send,
                recv_sem=h_recv,
                device_id=sibling,
                device_id_type=MESH,
            )
            half.start()
            half.wait_recv()

            def scatter(dx, dy):
                return pltpu.make_async_remote_copy(
                    src_ref=dsend.at[plane(dx, dy)],
                    dst_ref=drecv.at[dx * NY + dy],
                    send_sem=d_send.at[dx * NY + dy],
                    recv_sem=d_recv.at[dx * NY + dy],
                    device_id=(plane(dx, dy) * 2 + core, z),
                    device_id_type=MESH,
                )

            for dx, dy in STEPS:
                to = plane(dx, dy)
                dsend[to] = (halves[core, to] + sib[to]).astype(BF16)
                scatter(dx, dy).start()

    stores = [
        pltpu.make_async_copy(src, dst, out_sem.at[i])
        for i, (src, dst) in enumerate(
            (
                (gg, gate_grad), (ug, up_grad), (dg, down_grad), (mine.at[0], mixed), (mine.at[1], input_grad)
            )
        )
    ]
    for store in stores[:3]:
        store.start()
    for dx, dy in STEPS:
        gather(dx, dy, x, y).wait_send()
    for dx in COLUMNS:
        forward(dx, core).wait_send()
    for u in range(LANES):
        for k in sum_trees[u]:
            sum_copy(u, k).wait_send()
        for k in spread_trees[u]:
            spread_copy(u, k, z).wait_send()
    half.wait_send()
    total = halves[core, chip] + sib[chip]
    for dx, dy in reversed(STEPS):
        scatter(dx, dy).wait_recv()
        total += drecv[dx * NY + dy].astype(F32)
    mine[0] = total[0:8].astype(BF16)
    mine[1] = total[8:16].astype(BF16)
    for store in stores[3:]:
        store.start()
    for dx, dy in STEPS:
        scatter(dx, dy).wait_send()
    for store in stores:
        store.wait()


def hand_on(pieces, *refs):
    sources, targets, held, (in_sem, out_sem) = refs[:5], refs[5:10], refs[10:15], refs[15:]

    def rows(ref, j, n):
        return ref if n == ref.shape[0] else ref.at[pl.ds(j * n, n)]

    loads = [
        pltpu.make_async_copy(rows(sources[i], j, n), rows(held[i], j, n), in_sem.at[p])
        for p, (i, j, n) in enumerate(pieces)
    ]
    stores = [
        pltpu.make_async_copy(rows(held[i], j, n), rows(targets[i], j, n), out_sem.at[p])
        for p, (i, j, n) in enumerate(pieces)
    ]
    for load in loads:
        load.start()
    for load, store in zip(loads, stores):
        load.wait()
        store.start()
    for store in stores:
        store.wait()


def shards(tokens, gate_weight, up_weight, down_weight, out_grad):
    sum_trees, wide, spread_trees = trees()
    order, _ = plan(sum_trees, wide, spread_trees)
    anywhere = pl.BlockSpec(memory_space=pl.ANY)
    dma = pltpu.SemaphoreType.DMA
    shape = jax.ShapeDtypeStruct
    outs = pl.pallas_call(
        functools.partial(kernel, sum_trees, wide, spread_trees, order),
        out_shape=(
            shape((8, 512), BF16),
            shape((8, 512), BF16),
            shape((512, 768), BF16),
            shape((512, 768), BF16),
            shape((768, 512), BF16),
        ),
        in_specs=[anywhere] * 5,
        out_specs=(anywhere,) * 5,
        scratch_shapes=[
            pltpu.VMEM((2, 8, 512), BF16),
            pltpu.VMEM((2, 8, 512), BF16),
            pltpu.VMEM((512, 768), BF16),
            pltpu.VMEM((512, 768), BF16),
            pltpu.VMEM((768, 512), BF16),
            pltpu.VMEM((2, NX, NY, 16, 512), BF16),
            pltpu.VMEM((256, 512), BF16),
            pltpu.VMEM((256, 512), BF16),
            pltpu.VMEM((LANES, NZ, 16, 3 * W), F32),
            pltpu.VMEM((LANES, NZ - 1, 16, 3 * W), F32),
            pltpu.VMEM((LANES, NZ - 1, 16, 3 * W), BF16),
            pltpu.VMEM((LANES, NZ - 1, 16, 3 * W), BF16),
            pltpu.VMEM((LANES, NZ, 16, 3 * W), BF16),
            pltpu.VMEM((2, 16, 16, 512), F32),
            pltpu.VMEM((16, 16, 512), F32),
            pltpu.VMEM((16, 16, 512), BF16),
            pltpu.VMEM((16, 16, 512), BF16),
            pltpu.VMEM((512, 768), BF16),
            pltpu.VMEM((512, 768), BF16),
            pltpu.VMEM((768, 512), BF16),
            dma((5,)), dma((5,)),
            dma((16,)), dma((16,)), dma((4,)), dma((4,)),
            dma((LANES, NZ - 1)), dma((LANES, NZ - 1)),
            dma((LANES, NZ - 1)), dma((LANES, NZ - 1)),
            dma, dma, dma((16,)), dma((16,)),
        ],
        compiler_params=pltpu.CompilerParams(
            collective_id=0, has_side_effects=True, vmem_limit_bytes=62 * 2**20
        ),
    )(tokens, gate_weight, up_weight, down_weight, out_grad)
    pieces = [(i, 0, o.shape[0]) for i, o in enumerate(outs[:2])]
    pieces += [(i, j, o.shape[0] // 4) for i, o in enumerate(outs) if i > 1 for j in range(4)]
    return pl.pallas_call(
        functools.partial(hand_on, pieces),
        out_shape=tuple(shape(o.shape, o.dtype) for o in outs),
        in_specs=[anywhere] * 5,
        out_specs=(anywhere,) * 5,
        scratch_shapes=[pltpu.VMEM(o.shape, o.dtype) for o in outs]
        + [dma((len(pieces),)), dma((len(pieces),))],
    )(*outs)


def solution(mesh):
    return jax.shard_map(
        shards,
        mesh=mesh,
        in_specs=(
            P("row", "col"),
            P("col", "row"),
            P("col", "row"),
            P("row", "col"),
            P("row", "col"),
        ),
        out_specs=(
            P("row", "col"),
            P("row", "col"),
            P("col", "row"),
            P("col", "row"),
            P("row", "col"),
        ),
        check_vma=False,
    )
```

```python
import functools

import jax
import jax.numpy as jnp
from jax import lax
from jax.experimental import pallas as pl
from jax.experimental.pallas import tpu as pltpu
from jax.sharding import PartitionSpec as P

MESH = pl.DeviceIdType.MESH
F32, BF16 = jnp.float32, jnp.bfloat16
NZ, NX, NY = 16, 4, 4
LANES, W = 3, 256

SUM_FAR = {1: 0, 2: 1, 3: 2, 4: 3, 5: 6, 6: 3, 7: 6, 8: 6}
SUM_NEAR = {1: 0, 2: 1, 3: 2, 4: 5, 5: 2, 6: 5, 7: 5}
WIDE_FAR, WIDE_NEAR = (1, 2, 3), (1, 2)
SPREAD_FAR = {1: 0, 2: 0, 3: 2, 4: 2, 5: 4, 6: 4, 7: 6, 8: 6}
SPREAD_NEAR = {1: 0, 2: 0, 3: 2, 4: 2, 5: 4, 6: 4, 7: 6}
RATE, BURST, FIXED, HOP = 95.0, 130.0, 2.35, 0.65


def two_sided(far, near, way):
    return {**{way * k: way * p for k, p in far.items()}, **{-way * k: -way * p for k, p in near.items()}}


def sides(u):
    return 1 if u % 2 == 0 else -1


def trees():
    sums = [two_sided(SUM_FAR, SUM_NEAR, sides(u)) for u in range(LANES)]
    wide = [
        {sides(u) * k for k in WIDE_FAR} | {-sides(u) * k for k in WIDE_NEAR} for u in range(LANES)
    ]
    spreads = [two_sided(SPREAD_FAR, SPREAD_NEAR, -sides(u)) for u in range(LANES)]
    return sums, wide, spreads


def children(tree, k):
    return sorted((c for c, p in tree.items() if p == k), key=lambda c: -abs(c - k))


def plan(sum_trees, wide, spread_trees):
    kb = 72.0 / LANES
    free = {1: 0.0, -1: 0.0}
    arrive = {}
    clock = 0.0
    order = []

    def send(key, dist, kb, now):
        way = 1 if dist > 0 else -1
        hops = abs(dist)
        begin = max(free[way], now)
        free[way] = begin + kb * 2 * hops / RATE
        arrive[key] = begin + kb * 2 / BURST + FIXED + HOP * hops

    todo = []
    for u in range(LANES):
        todo.append(("mm", u, 0))
        todo += [("sum", u, k) for k in sorted(sum_trees[u], key=lambda k: -abs(k - sum_trees[u][k]))]
        todo.append(("own", u, 0))
        todo += [("spread", u, k) for k in spread_trees[u] if children(spread_trees[u], k)]
        todo.append(("fin", u, 0))
        todo.append(("grad", u, 0))
    done = set()
    cost = {"mm": 0.33, "sum": 0.06, "own": 0.1, "spread": 0.04, "fin": 0.3, "grad": 0.17}
    last = {"mm": 0, "grad": 1e6}

    def ready(task):
        kind, u, k = task
        if kind == "mm":
            return 0.0 if u == 0 or ("mm", u - 1, 0) in done else None
        if kind == "sum" or kind == "own":
            if ("mm", u, 0) not in done:
                return None
            keys = [("sum", u, c) for c in children(sum_trees[u], k)]
        elif kind == "spread":
            keys = [("spread", u, k)]
        elif kind == "fin":
            if ("own", u, 0) not in done:
                return None
            keys = [("spread", u, c) for c in spread_trees[u]]
        else:
            return 0.0 if ("fin", u, 0) in done else None
        if any(key not in arrive for key in keys):
            return None
        return max([0.0] + [arrive[key] for key in keys])

    while todo:
        best = None
        for task in todo:
            at = ready(task)
            if at is None:
                continue
            rank = (max(at, clock) + last.get(task[0], 0.0), task[1], at)
            if best is None or rank < best[0]:
                best = (rank, task, at)
        _, task, at = best
        kind, u, k = task
        clock = max(clock, at) + cost[kind]
        if kind == "sum":
            send(("sum", u, k), k - sum_trees[u][k], kb * (2 if k in wide[u] else 1), clock)
        elif kind in ("own", "spread"):
            for c in children(spread_trees[u], k):
                send(("spread", u, c), c - k, kb, clock)
        order.append(task)
        done.add(task)
        todo.remove(task)
    return order, clock


def offsets(sum_trees, spread_trees):
    found = set()
    for tree in sum_trees:
        found |= {(k - p) % NZ for k, p in tree.items()}
    for tree in spread_trees:
        found |= {(k - p) % NZ for k, p in tree.items()}
    found |= {(-o) % NZ for o in found}
    return sorted(found)


def torus(step):
    return min(step, 4 - step)


STEPS = sorted(
    [(dx, dy) for dx in range(NX) for dy in range(NY) if (dx, dy) != (0, 0)],
    key=lambda s: -(torus(s[0]) + torus(s[1])),
)
COLUMNS = [0, 1, 3, 2]


def dot(a, b, dims):
    return lax.dot_general(a, b, (dims, ((), ())), preferred_element_type=F32)


NN, NT, TN = ((1,), (0,)), ((1,), (1,)), ((0,), (0,))


def kernel(
    sum_trees, wide, spread_trees, order,
    tok, gate_w, up_w, down_w, og,
    mixed, input_grad, gate_grad, up_grad, down_grad,
    own, mine, gw, uw, dw, slabs, xs, gs, part, slot, low_out, low_in, acts, halves, sib, dsend, drecv, gg, ug, dg,
    w_sem, out_sem, a_send, a_recv, f_send, f_recv,
    sum_send, sum_recv, spread_send, spread_recv, h_send, h_recv, d_send, d_recv,
):
    row, z = lax.axis_index("row"), lax.axis_index("col")
    core, chip = row % 2, row // 2
    x, y = chip // NY, chip % NY
    sibling = (chip * 2 + 1 - core, z)

    def plane(dx, dy):
        return ((x + dx) % NX) * NY + (y + dy) % NY

    barrier = pltpu.get_barrier_semaphore()
    around = offsets(sum_trees, spread_trees)
    for dx, dy in STEPS:
        pl.semaphore_signal(
            barrier, inc=1, device_id=(plane(dx, dy) * 2 + core, z), device_id_type=MESH
        )
    for o in around:
        pl.semaphore_signal(barrier, inc=1, device_id=(row, (z + o) % NZ), device_id_type=MESH)
    pl.semaphore_signal(barrier, inc=1, device_id=sibling, device_id_type=MESH)
    loads = [
        pltpu.make_async_copy(src, dst, w_sem.at[i])
        for i, (src, dst) in enumerate(
            ((gate_w, gw), (up_w, uw), (down_w, dw), (tok, own.at[0]), (og, own.at[1]))
        )
    ]
    for load in reversed(loads):
        load.start()
    for load in loads[3:]:
        load.wait()
    slabs[core, x, y] = jnp.concatenate([own[0].astype(F32), own[1].astype(F32)], axis=0).astype(BF16)
    pl.semaphore_wait(barrier, len(STEPS) + len(around) + 1)

    def gather(dx, dy, from_x, from_y):
        return pltpu.make_async_remote_copy(
            src_ref=slabs.at[core, from_x, from_y],
            dst_ref=slabs.at[core, from_x, from_y],
            send_sem=a_send.at[dx * NY + dy],
            recv_sem=a_recv.at[dx * NY + dy],
            device_id=(plane(dx, dy) * 2 + core, z),
            device_id_type=MESH,
        )

    def forward(dx, which):
        return pltpu.make_async_remote_copy(
            src_ref=slabs.at[which, (x - dx) % NX],
            dst_ref=slabs.at[which, (x - dx) % NX],
            send_sem=f_send.at[dx],
            recv_sem=f_recv.at[dx],
            device_id=sibling,
            device_id_type=MESH,
        )

    for dx, dy in STEPS:
        gather(dx, dy, x, y).start()
    for dx in COLUMNS:
        for dy in range(NY):
            if (dx, dy) in STEPS:
                gather(dx, dy, (x - dx) % NX, (y - dy) % NY).wait_recv()
        forward(dx, core).start()
    def unpack(which):
        rows, place = slabs[which].astype(F32), pl.ds(which * 128, 128)
        xs[place, :] = rows[:, :, 0:8, :].reshape(128, 512).astype(BF16)
        gs[place, :] = rows[:, :, 8:16, :].reshape(128, 512).astype(BF16)

    unpack(core)
    for load in loads[:3]:
        load.wait()
    for dx in COLUMNS:
        forward(dx, 1 - core).wait_recv()
    unpack(1 - core)

    def index(tree, k):
        return sorted(tree).index(k)

    def sum_copy(u, k):
        o = k - sum_trees[u][k]
        i = index(sum_trees[u], k)
        return pltpu.make_async_remote_copy(
            src_ref=part.at[u, (z + k) % NZ] if k in wide[u] else low_out.at[u, i],
            dst_ref=slot.at[u, i] if k in wide[u] else low_in.at[u, i],
            send_sem=sum_send.at[u, i],
            recv_sem=sum_recv.at[u, i],
            device_id=(row, (z + o) % NZ),
            device_id_type=MESH,
        )

    def spread_copy(u, c, chunk):
        o = c - spread_trees[u][c]
        i = index(spread_trees[u], c)
        return pltpu.make_async_remote_copy(
            src_ref=acts.at[u, chunk],
            dst_ref=acts.at[u, chunk],
            send_sem=spread_send.at[u, i],
            recv_sem=spread_recv.at[u, i],
            device_id=(row, (z + o) % NZ),
            device_id_type=MESH,
        )

    def gathered(u, k, total):
        for c in children(sum_trees[u], k):
            sum_copy(u, c).wait_recv()
            i = index(sum_trees[u], c)
            total += slot[u, i] if c in wide[u] else low_in[u, i].astype(F32)
        return total

    def spread_wait(u, k):
        spread_copy(u, k, (z - k) % NZ).wait_recv()

    begun = False
    for kind, u, k in order:
        unit = pl.ds(u * W, W)
        if kind == "mm":
            part[u, :, :, 0:W] = dot(xs[...], gw[:, unit], NN).reshape(NZ, 16, W)
            part[u, :, :, W : 2 * W] = dot(xs[...], uw[:, unit], NN).reshape(NZ, 16, W)
            part[u, :, :, 2 * W : 3 * W] = dot(gs[...], dw[unit, :], NT).reshape(NZ, 16, W)
        elif kind == "sum":
            chunk = (z + k) % NZ
            total = gathered(u, k, part[u, chunk])
            if k not in wide[u]:
                low_out[u, index(sum_trees[u], k)] = total.astype(BF16)
            elif children(sum_trees[u], k):
                part[u, chunk] = total
            sum_copy(u, k).start()
        elif kind == "own":
            total = gathered(u, 0, part[u, z])
            gate, up, hidden_grad = total[:, 0:W], total[:, W : 2 * W], total[:, 2 * W :]
            sig = jax.nn.sigmoid(gate)
            swish = gate * sig
            acts[u, z, :, 0:W] = (swish * up).astype(BF16)
            acts[u, z, :, W : 2 * W] = (
                hidden_grad * up * sig * (1.0 + gate * (1.0 - sig))
            ).astype(BF16)
            acts[u, z, :, 2 * W : 3 * W] = (hidden_grad * swish).astype(BF16)
            for c in children(spread_trees[u], 0):
                spread_copy(u, c, z).start()
        elif kind == "spread":
            spread_wait(u, k)
            for c in children(spread_trees[u], k):
                spread_copy(u, c, (z - k) % NZ).start()
        elif kind == "fin":
            for c in spread_trees[u]:
                if not children(spread_trees[u], c):
                    spread_wait(u, c)
            hidden = acts[u, :, :, 0:W].reshape(256, W)
            gate_delta = acts[u, :, :, W : 2 * W].reshape(256, W)
            up_delta = acts[u, :, :, 2 * W : 3 * W].reshape(256, W)
            out = dot(hidden, dw[unit, :], NN).reshape(2, 16, 8, 512)
            back = (dot(gate_delta, gw[:, unit], NT) + dot(up_delta, uw[:, unit], NT)).reshape(
                2, 16, 8, 512
            )
            if begun:
                out += halves[:, :, 0:8, :]
                back += halves[:, :, 8:16, :]
            halves[:, :, 0:8, :] = out
            halves[:, :, 8:16, :] = back
            begun = True
        else:
            hidden = acts[u, :, :, 0:W].reshape(256, W)
            gate_delta = acts[u, :, :, W : 2 * W].reshape(256, W)
            up_delta = acts[u, :, :, 2 * W : 3 * W].reshape(256, W)
            gg[:, unit] = dot(xs[...], gate_delta, TN).astype(BF16)
            ug[:, unit] = dot(xs[...], up_delta, TN).astype(BF16)
            dg[unit, :] = dot(hidden, gs[...], TN).astype(BF16)
        if kind == "fin" and (kind, u, k) == [t for t in order if t[0] == "fin"][-1]:
            def half(dx):
                chips = pl.ds((x + dx) % NX * NY, NY)
                return pltpu.make_async_remote_copy(
                    src_ref=halves.at[1 - core, chips],
                    dst_ref=sib.at[chips],
                    send_sem=h_send.at[dx],
                    recv_sem=h_recv.at[dx],
                    device_id=sibling,
                    device_id_type=MESH,
                )

            for dx in reversed(COLUMNS):
                half(dx).start()

            def scatter(dx, dy):
                return pltpu.make_async_remote_copy(
                    src_ref=dsend.at[plane(dx, dy)],
                    dst_ref=drecv.at[dx * NY + dy],
                    send_sem=d_send.at[dx * NY + dy],
                    recv_sem=d_recv.at[dx * NY + dy],
                    device_id=(plane(dx, dy) * 2 + core, z),
                    device_id_type=MESH,
                )

            for dx in reversed(COLUMNS):
                half(dx).wait_recv()
                for dy in (2, 1, 3, 0):
                    if (dx, dy) in STEPS:
                        to = plane(dx, dy)
                        dsend[to] = (halves[core, to] + sib[to]).astype(BF16)
                        scatter(dx, dy).start()

    stores = [
        pltpu.make_async_copy(src, dst, out_sem.at[i])
        for i, (src, dst) in enumerate(
            (
                (gg, gate_grad), (ug, up_grad), (dg, down_grad), (mine.at[0], mixed), (mine.at[1], input_grad)
            )
        )
    ]
    for store in stores[:3]:
        store.start()
    for dx, dy in STEPS:
        gather(dx, dy, x, y).wait_send()
    for dx in COLUMNS:
        forward(dx, core).wait_send()
    for u in range(LANES):
        for k in sum_trees[u]:
            sum_copy(u, k).wait_send()
        for k in spread_trees[u]:
            spread_copy(u, k, z).wait_send()
    for dx in COLUMNS:
        half(dx).wait_send()
    total = halves[core, chip] + sib[chip]
    for dx, dy in reversed(STEPS):
        scatter(dx, dy).wait_recv()
        total += drecv[dx * NY + dy].astype(F32)
    mine[0] = total[0:8].astype(BF16)
    mine[1] = total[8:16].astype(BF16)
    for store in stores[3:]:
        store.start()
    for dx, dy in STEPS:
        scatter(dx, dy).wait_send()
    for store in stores:
        store.wait()


def hand_on(pieces, *refs):
    sources, targets, held, (in_sem, out_sem) = refs[:5], refs[5:10], refs[10:15], refs[15:]

    def rows(ref, j, n):
        return ref if n == ref.shape[0] else ref.at[pl.ds(j * n, n)]

    loads = [
        pltpu.make_async_copy(rows(sources[i], j, n), rows(held[i], j, n), in_sem.at[p])
        for p, (i, j, n) in enumerate(pieces)
    ]
    stores = [
        pltpu.make_async_copy(rows(held[i], j, n), rows(targets[i], j, n), out_sem.at[p])
        for p, (i, j, n) in enumerate(pieces)
    ]
    for load in loads:
        load.start()
    for load, store in zip(loads, stores):
        load.wait()
        store.start()
    for store in stores:
        store.wait()


def shards(tokens, gate_weight, up_weight, down_weight, out_grad):
    sum_trees, wide, spread_trees = trees()
    order, _ = plan(sum_trees, wide, spread_trees)
    anywhere = pl.BlockSpec(memory_space=pl.ANY)
    dma = pltpu.SemaphoreType.DMA
    shape = jax.ShapeDtypeStruct
    outs = pl.pallas_call(
        functools.partial(kernel, sum_trees, wide, spread_trees, order),
        out_shape=(
            shape((8, 512), BF16),
            shape((8, 512), BF16),
            shape((512, 768), BF16),
            shape((512, 768), BF16),
            shape((768, 512), BF16),
        ),
        in_specs=[anywhere] * 5,
        out_specs=(anywhere,) * 5,
        scratch_shapes=[
            pltpu.VMEM((2, 8, 512), BF16),
            pltpu.VMEM((2, 8, 512), BF16),
            pltpu.VMEM((512, 768), BF16),
            pltpu.VMEM((512, 768), BF16),
            pltpu.VMEM((768, 512), BF16),
            pltpu.VMEM((2, NX, NY, 16, 512), BF16),
            pltpu.VMEM((256, 512), BF16),
            pltpu.VMEM((256, 512), BF16),
            pltpu.VMEM((LANES, NZ, 16, 3 * W), F32),
            pltpu.VMEM((LANES, NZ - 1, 16, 3 * W), F32),
            pltpu.VMEM((LANES, NZ - 1, 16, 3 * W), BF16),
            pltpu.VMEM((LANES, NZ - 1, 16, 3 * W), BF16),
            pltpu.VMEM((LANES, NZ, 16, 3 * W), BF16),
            pltpu.VMEM((2, 16, 16, 512), F32),
            pltpu.VMEM((16, 16, 512), F32),
            pltpu.VMEM((16, 16, 512), BF16),
            pltpu.VMEM((16, 16, 512), BF16),
            pltpu.VMEM((512, 768), BF16),
            pltpu.VMEM((512, 768), BF16),
            pltpu.VMEM((768, 512), BF16),
            dma((5,)), dma((5,)),
            dma((16,)), dma((16,)), dma((4,)), dma((4,)),
            dma((LANES, NZ - 1)), dma((LANES, NZ - 1)),
            dma((LANES, NZ - 1)), dma((LANES, NZ - 1)),
            dma((4,)), dma((4,)), dma((16,)), dma((16,)),
        ],
        compiler_params=pltpu.CompilerParams(
            collective_id=0, has_side_effects=True, vmem_limit_bytes=62 * 2**20
        ),
    )(tokens, gate_weight, up_weight, down_weight, out_grad)
    pieces = [(i, 0, o.shape[0]) for i, o in enumerate(outs[:2])]
    pieces += [(i, j, o.shape[0] // 4) for i, o in enumerate(outs) if i > 1 for j in range(4)]
    return pl.pallas_call(
        functools.partial(hand_on, pieces),
        out_shape=tuple(shape(o.shape, o.dtype) for o in outs),
        in_specs=[anywhere] * 5,
        out_specs=(anywhere,) * 5,
        scratch_shapes=[pltpu.VMEM(o.shape, o.dtype) for o in outs]
        + [dma((len(pieces),)), dma((len(pieces),))],
    )(*outs)


def solution(mesh):
    return jax.shard_map(
        shards,
        mesh=mesh,
        in_specs=(
            P("row", "col"),
            P("col", "row"),
            P("col", "row"),
            P("row", "col"),
            P("row", "col"),
        ),
        out_specs=(
            P("row", "col"),
            P("row", "col"),
            P("col", "row"),
            P("col", "row"),
            P("row", "col"),
        ),
        check_vma=False,
    )
```

```python
import functools

import jax
import jax.numpy as jnp
from jax import lax
from jax.experimental import pallas as pl
from jax.experimental.pallas import tpu as pltpu
from jax.sharding import PartitionSpec as P

MESH = pl.DeviceIdType.MESH
F32, BF16 = jnp.float32, jnp.bfloat16
NZ, NX, NY = 16, 4, 4
LANES, W = 3, 256

SUM_FAR = {1: 0, 2: 1, 3: 2, 4: 3, 5: 6, 6: 3, 7: 6, 8: 6}
SUM_NEAR = {1: 0, 2: 1, 3: 2, 4: 5, 5: 2, 6: 5, 7: 5}
WIDE_FAR, WIDE_NEAR = (1, 2, 3), (1, 2)
SPREAD_FAR = {1: 0, 2: 0, 3: 2, 4: 2, 5: 4, 6: 4, 7: 6, 8: 6}
SPREAD_NEAR = {1: 0, 2: 0, 3: 2, 4: 2, 5: 4, 6: 4, 7: 6}
RATE, BURST, FIXED, HOP = 95.0, 130.0, 2.35, 0.65


def two_sided(far, near, way):
    return {**{way * k: way * p for k, p in far.items()}, **{-way * k: -way * p for k, p in near.items()}}


def sides(u):
    return 1 if u % 2 == 0 else -1


def trees():
    sums = [two_sided(SUM_FAR, SUM_NEAR, sides(u)) for u in range(LANES)]
    wide = [
        {sides(u) * k for k in WIDE_FAR} | {-sides(u) * k for k in WIDE_NEAR} for u in range(LANES)
    ]
    spreads = [two_sided(SPREAD_FAR, SPREAD_NEAR, -sides(u)) for u in range(LANES)]
    return sums, wide, spreads


def children(tree, k):
    return sorted((c for c, p in tree.items() if p == k), key=lambda c: -abs(c - k))


def plan(sum_trees, wide, spread_trees):
    kb = 72.0 / LANES
    free = {1: 0.0, -1: 0.0}
    arrive = {}
    clock = 0.0
    order = []

    def send(key, dist, kb, now):
        way = 1 if dist > 0 else -1
        hops = abs(dist)
        begin = max(free[way], now)
        free[way] = begin + kb * 2 * hops / RATE
        arrive[key] = begin + kb * 2 / BURST + FIXED + HOP * hops

    todo = []
    for u in range(LANES):
        todo.append(("mm", u, 0))
        todo += [("sum", u, k) for k in sorted(sum_trees[u], key=lambda k: -abs(k - sum_trees[u][k]))]
        todo.append(("own", u, 0))
        todo += [("spread", u, k) for k in spread_trees[u] if children(spread_trees[u], k)]
        todo.append(("fin", u, 0))
        todo.append(("grad", u, 0))
    done = set()
    cost = {"mm": 0.33, "sum": 0.06, "own": 0.1, "spread": 0.04, "fin": 0.3, "grad": 0.17}
    last = {"mm": 0, "grad": 1e6}

    def ready(task):
        kind, u, k = task
        if kind == "mm":
            return 0.0 if u == 0 or ("mm", u - 1, 0) in done else None
        if kind == "sum" or kind == "own":
            if ("mm", u, 0) not in done:
                return None
            keys = [("sum", u, c) for c in children(sum_trees[u], k)]
        elif kind == "spread":
            keys = [("spread", u, k)]
        elif kind == "fin":
            if ("own", u, 0) not in done:
                return None
            keys = [("spread", u, c) for c in spread_trees[u]]
        else:
            return 0.0 if ("fin", u, 0) in done else None
        if any(key not in arrive for key in keys):
            return None
        return max([0.0] + [arrive[key] for key in keys])

    while todo:
        best = None
        for task in todo:
            at = ready(task)
            if at is None:
                continue
            rank = (max(at, clock) + last.get(task[0], 0.0), task[1], at)
            if best is None or rank < best[0]:
                best = (rank, task, at)
        _, task, at = best
        kind, u, k = task
        clock = max(clock, at) + cost[kind]
        if kind == "sum":
            send(("sum", u, k), k - sum_trees[u][k], kb * (2 if k in wide[u] else 1), clock)
        elif kind in ("own", "spread"):
            for c in children(spread_trees[u], k):
                send(("spread", u, c), c - k, kb, clock)
        order.append(task)
        done.add(task)
        todo.remove(task)
    return order, clock


def offsets(sum_trees, spread_trees):
    found = set()
    for tree in sum_trees:
        found |= {(k - p) % NZ for k, p in tree.items()}
    for tree in spread_trees:
        found |= {(k - p) % NZ for k, p in tree.items()}
    found |= {(-o) % NZ for o in found}
    return sorted(found)


def torus(step):
    return min(step, 4 - step)


STEPS = sorted(
    [(dx, dy) for dx in range(NX) for dy in range(NY) if (dx, dy) != (0, 0)],
    key=lambda s: -(torus(s[0]) + torus(s[1])),
)
COLUMNS = [0, 1, 3, 2]


def dot(a, b, dims):
    return lax.dot_general(a, b, (dims, ((), ())), preferred_element_type=F32)


NN, NT, TN = ((1,), (0,)), ((1,), (1,)), ((0,), (0,))


def kernel(
    sum_trees, wide, spread_trees, order,
    rows, gate_w, up_w, down_w,
    mixed, input_grad, gate_grad, up_grad, down_grad,
    mine, gw, uw, dw, slabs, xs, gs, part, slot, low_out, low_in, acts, halves, sib, dsend, drecv, gg, ug, dg,
    w_sem, out_sem, a_send, a_recv, f_send, f_recv,
    sum_send, sum_recv, spread_send, spread_recv, h_send, h_recv, d_send, d_recv,
):
    row, z = lax.axis_index("row"), lax.axis_index("col")
    core, chip = row % 2, row // 2
    x, y = chip // NY, chip % NY
    sibling = (chip * 2 + 1 - core, z)

    def plane(dx, dy):
        return ((x + dx) % NX) * NY + (y + dy) % NY

    barrier = pltpu.get_barrier_semaphore()
    around = offsets(sum_trees, spread_trees)
    for dx, dy in STEPS:
        pl.semaphore_signal(
            barrier, inc=1, device_id=(plane(dx, dy) * 2 + core, z), device_id_type=MESH
        )
    for o in around:
        pl.semaphore_signal(barrier, inc=1, device_id=(row, (z + o) % NZ), device_id_type=MESH)
    pl.semaphore_signal(barrier, inc=1, device_id=sibling, device_id_type=MESH)
    loads = [
        pltpu.make_async_copy(src, dst, w_sem.at[i])
        for i, (src, dst) in enumerate(
            ((gate_w, gw), (up_w, uw), (down_w, dw), (rows, slabs.at[core, x, y]))
        )
    ]
    for load in reversed(loads):
        load.start()
    for load in loads[3:]:
        load.wait()
    pl.semaphore_wait(barrier, len(STEPS) + len(around) + 1)

    def gather(dx, dy, from_x, from_y):
        return pltpu.make_async_remote_copy(
            src_ref=slabs.at[core, from_x, from_y],
            dst_ref=slabs.at[core, from_x, from_y],
            send_sem=a_send.at[dx * NY + dy],
            recv_sem=a_recv.at[dx * NY + dy],
            device_id=(plane(dx, dy) * 2 + core, z),
            device_id_type=MESH,
        )

    def forward(dx, which):
        return pltpu.make_async_remote_copy(
            src_ref=slabs.at[which, (x - dx) % NX],
            dst_ref=slabs.at[which, (x - dx) % NX],
            send_sem=f_send.at[dx],
            recv_sem=f_recv.at[dx],
            device_id=sibling,
            device_id_type=MESH,
        )

    for dx, dy in STEPS:
        gather(dx, dy, x, y).start()
    for dx in COLUMNS:
        for dy in range(NY):
            if (dx, dy) in STEPS:
                gather(dx, dy, (x - dx) % NX, (y - dy) % NY).wait_recv()
        forward(dx, core).start()
    def unpack(which):
        rows, place = slabs[which].astype(F32), pl.ds(which * 128, 128)
        xs[place, :] = rows[:, :, 0:8, :].reshape(128, 512).astype(BF16)
        gs[place, :] = rows[:, :, 8:16, :].reshape(128, 512).astype(BF16)

    unpack(core)
    for load in loads[:3]:
        load.wait()
    for dx in COLUMNS:
        forward(dx, 1 - core).wait_recv()
    unpack(1 - core)

    def index(tree, k):
        return sorted(tree).index(k)

    def sum_copy(u, k):
        o = k - sum_trees[u][k]
        i = index(sum_trees[u], k)
        return pltpu.make_async_remote_copy(
            src_ref=part.at[u, (z + k) % NZ] if k in wide[u] else low_out.at[u, i],
            dst_ref=slot.at[u, i] if k in wide[u] else low_in.at[u, i],
            send_sem=sum_send.at[u, i],
            recv_sem=sum_recv.at[u, i],
            device_id=(row, (z + o) % NZ),
            device_id_type=MESH,
        )

    def spread_copy(u, c, chunk):
        o = c - spread_trees[u][c]
        i = index(spread_trees[u], c)
        return pltpu.make_async_remote_copy(
            src_ref=acts.at[u, chunk],
            dst_ref=acts.at[u, chunk],
            send_sem=spread_send.at[u, i],
            recv_sem=spread_recv.at[u, i],
            device_id=(row, (z + o) % NZ),
            device_id_type=MESH,
        )

    def gathered(u, k, total):
        for c in children(sum_trees[u], k):
            sum_copy(u, c).wait_recv()
            i = index(sum_trees[u], c)
            total += slot[u, i] if c in wide[u] else low_in[u, i].astype(F32)
        return total

    def spread_wait(u, k):
        spread_copy(u, k, (z - k) % NZ).wait_recv()

    begun = False
    for kind, u, k in order:
        unit = pl.ds(u * W, W)
        if kind == "mm":
            part[u, :, :, 0:W] = dot(xs[...], gw[:, unit], NN).reshape(NZ, 16, W)
            part[u, :, :, W : 2 * W] = dot(xs[...], uw[:, unit], NN).reshape(NZ, 16, W)
            part[u, :, :, 2 * W : 3 * W] = dot(gs[...], dw[unit, :], NT).reshape(NZ, 16, W)
        elif kind == "sum":
            chunk = (z + k) % NZ
            total = gathered(u, k, part[u, chunk])
            if k not in wide[u]:
                low_out[u, index(sum_trees[u], k)] = total.astype(BF16)
            elif children(sum_trees[u], k):
                part[u, chunk] = total
            sum_copy(u, k).start()
        elif kind == "own":
            total = gathered(u, 0, part[u, z])
            gate, up, hidden_grad = total[:, 0:W], total[:, W : 2 * W], total[:, 2 * W :]
            sig = jax.nn.sigmoid(gate)
            swish = gate * sig
            acts[u, z, :, 0:W] = (swish * up).astype(BF16)
            acts[u, z, :, W : 2 * W] = (
                hidden_grad * up * sig * (1.0 + gate * (1.0 - sig))
            ).astype(BF16)
            acts[u, z, :, 2 * W : 3 * W] = (hidden_grad * swish).astype(BF16)
            for c in children(spread_trees[u], 0):
                spread_copy(u, c, z).start()
        elif kind == "spread":
            spread_wait(u, k)
            for c in children(spread_trees[u], k):
                spread_copy(u, c, (z - k) % NZ).start()
        elif kind == "fin":
            for c in spread_trees[u]:
                if not children(spread_trees[u], c):
                    spread_wait(u, c)
            hidden = acts[u, :, :, 0:W].reshape(256, W)
            gate_delta = acts[u, :, :, W : 2 * W].reshape(256, W)
            up_delta = acts[u, :, :, 2 * W : 3 * W].reshape(256, W)
            out = dot(hidden, dw[unit, :], NN).reshape(2, 16, 8, 512)
            back = (dot(gate_delta, gw[:, unit], NT) + dot(up_delta, uw[:, unit], NT)).reshape(
                2, 16, 8, 512
            )
            if begun:
                out += halves[:, :, 0:8, :]
                back += halves[:, :, 8:16, :]
            halves[:, :, 0:8, :] = out
            halves[:, :, 8:16, :] = back
            begun = True
        else:
            hidden = acts[u, :, :, 0:W].reshape(256, W)
            gate_delta = acts[u, :, :, W : 2 * W].reshape(256, W)
            up_delta = acts[u, :, :, 2 * W : 3 * W].reshape(256, W)
            gg[:, unit] = dot(xs[...], gate_delta, TN).astype(BF16)
            ug[:, unit] = dot(xs[...], up_delta, TN).astype(BF16)
            dg[unit, :] = dot(hidden, gs[...], TN).astype(BF16)
        if kind == "fin" and (kind, u, k) == [t for t in order if t[0] == "fin"][-1]:
            def half(dx):
                chips = pl.ds((x + dx) % NX * NY, NY)
                return pltpu.make_async_remote_copy(
                    src_ref=halves.at[1 - core, chips],
                    dst_ref=sib.at[chips],
                    send_sem=h_send.at[dx],
                    recv_sem=h_recv.at[dx],
                    device_id=sibling,
                    device_id_type=MESH,
                )

            for dx in reversed(COLUMNS):
                half(dx).start()

            def scatter(dx, dy):
                return pltpu.make_async_remote_copy(
                    src_ref=dsend.at[plane(dx, dy)],
                    dst_ref=drecv.at[dx * NY + dy],
                    send_sem=d_send.at[dx * NY + dy],
                    recv_sem=d_recv.at[dx * NY + dy],
                    device_id=(plane(dx, dy) * 2 + core, z),
                    device_id_type=MESH,
                )

            for dx in reversed(COLUMNS):
                half(dx).wait_recv()
                for dy in (2, 1, 3, 0):
                    if (dx, dy) in STEPS:
                        to = plane(dx, dy)
                        dsend[to] = (halves[core, to] + sib[to]).astype(BF16)
                        scatter(dx, dy).start()

    stores = [
        pltpu.make_async_copy(src, dst, out_sem.at[i])
        for i, (src, dst) in enumerate(
            (
                (gg, gate_grad), (ug, up_grad), (dg, down_grad), (mine.at[0], mixed), (mine.at[1], input_grad)
            )
        )
    ]
    for store in stores[:3]:
        store.start()
    for dx, dy in STEPS:
        gather(dx, dy, x, y).wait_send()
    for dx in COLUMNS:
        forward(dx, core).wait_send()
    for u in range(LANES):
        for k in sum_trees[u]:
            sum_copy(u, k).wait_send()
        for k in spread_trees[u]:
            spread_copy(u, k, z).wait_send()
    for dx in COLUMNS:
        half(dx).wait_send()
    total = halves[core, chip] + sib[chip]
    for dx, dy in reversed(STEPS):
        scatter(dx, dy).wait_recv()
        total += drecv[dx * NY + dy].astype(F32)
    mine[0] = total[0:8].astype(BF16)
    mine[1] = total[8:16].astype(BF16)
    for store in stores[3:]:
        store.start()
    for dx, dy in STEPS:
        scatter(dx, dy).wait_send()
    for store in stores:
        store.wait()


def hand_on(*refs):
    copies = [pltpu.make_async_copy(refs[i], refs[5 + i], refs[10].at[i]) for i in range(5)]
    for copy in copies:
        copy.start()
    for copy in copies:
        copy.wait()


def shards(tokens, gate_weight, up_weight, down_weight, out_grad):
    sum_trees, wide, spread_trees = trees()
    order, _ = plan(sum_trees, wide, spread_trees)
    anywhere = pl.BlockSpec(memory_space=pl.ANY)
    dma = pltpu.SemaphoreType.DMA
    shape = jax.ShapeDtypeStruct
    outs = pl.pallas_call(
        functools.partial(kernel, sum_trees, wide, spread_trees, order),
        out_shape=(
            shape((8, 512), BF16),
            shape((8, 512), BF16),
            shape((512, 768), BF16),
            shape((512, 768), BF16),
            shape((768, 512), BF16),
        ),
        in_specs=[anywhere] * 4,
        out_specs=(anywhere,) * 5,
        scratch_shapes=[
            pltpu.VMEM((2, 8, 512), BF16),
            pltpu.VMEM((512, 768), BF16),
            pltpu.VMEM((512, 768), BF16),
            pltpu.VMEM((768, 512), BF16),
            pltpu.VMEM((2, NX, NY, 16, 512), BF16),
            pltpu.VMEM((256, 512), BF16),
            pltpu.VMEM((256, 512), BF16),
            pltpu.VMEM((LANES, NZ, 16, 3 * W), F32),
            pltpu.VMEM((LANES, NZ - 1, 16, 3 * W), F32),
            pltpu.VMEM((LANES, NZ - 1, 16, 3 * W), BF16),
            pltpu.VMEM((LANES, NZ - 1, 16, 3 * W), BF16),
            pltpu.VMEM((LANES, NZ, 16, 3 * W), BF16),
            pltpu.VMEM((2, 16, 16, 512), F32),
            pltpu.VMEM((16, 16, 512), F32),
            pltpu.VMEM((16, 16, 512), BF16),
            pltpu.VMEM((16, 16, 512), BF16),
            pltpu.VMEM((512, 768), BF16),
            pltpu.VMEM((512, 768), BF16),
            pltpu.VMEM((768, 512), BF16),
            dma((5,)), dma((5,)),
            dma((16,)), dma((16,)), dma((4,)), dma((4,)),
            dma((LANES, NZ - 1)), dma((LANES, NZ - 1)),
            dma((LANES, NZ - 1)), dma((LANES, NZ - 1)),
            dma((4,)), dma((4,)), dma((16,)), dma((16,)),
        ],
        compiler_params=pltpu.CompilerParams(
            collective_id=0, has_side_effects=True, vmem_limit_bytes=205 * 2**18
        ),
    )(jnp.concatenate([tokens, out_grad], axis=0), gate_weight, up_weight, down_weight)
    return pl.pallas_call(
        hand_on,
        out_shape=tuple(shape(o.shape, o.dtype) for o in outs),
        in_specs=[pl.BlockSpec(memory_space=pltpu.VMEM)] * 5,
        out_specs=(anywhere,) * 5,
        scratch_shapes=[dma((5,))],
        compiler_params=pltpu.CompilerParams(vmem_limit_bytes=4 * 2**20),
    )(*outs)


def solution(mesh):
    return jax.shard_map(
        shards,
        mesh=mesh,
        in_specs=(
            P("row", "col"),
            P("col", "row"),
            P("col", "row"),
            P("row", "col"),
            P("row", "col"),
        ),
        out_specs=(
            P("row", "col"),
            P("row", "col"),
            P("col", "row"),
            P("col", "row"),
            P("row", "col"),
        ),
        check_vma=False,
    )
```

```python
import functools

import jax
import jax.numpy as jnp
from jax import lax
from jax.experimental import pallas as pl
from jax.experimental.pallas import tpu as pltpu
from jax.sharding import PartitionSpec as P

MESH = pl.DeviceIdType.MESH
F32, BF16 = jnp.float32, jnp.bfloat16
NZ, NX, NY = 16, 4, 4
LANES, W = 3, 256

SUM_FAR = {1: 0, 2: 1, 3: 2, 4: 3, 5: 6, 6: 3, 7: 6, 8: 6}
SUM_NEAR = {1: 0, 2: 1, 3: 2, 4: 5, 5: 2, 6: 5, 7: 5}
WIDE_FAR, WIDE_NEAR = (1, 2, 3), (1, 2)
SPREAD_FAR = {1: 0, 2: 0, 3: 2, 4: 2, 5: 4, 6: 4, 7: 6, 8: 6}
SPREAD_NEAR = {1: 0, 2: 0, 3: 2, 4: 2, 5: 4, 6: 4, 7: 6}
RATE, BURST, FIXED, HOP = 95.0, 130.0, 2.35, 0.65


def two_sided(far, near, way):
    return {**{way * k: way * p for k, p in far.items()}, **{-way * k: -way * p for k, p in near.items()}}


def sides(u):
    return 1 if u == 0 else -1


def trees():
    sums = [two_sided(SUM_FAR, SUM_NEAR, sides(u)) for u in range(LANES)]
    wide = [
        {sides(u) * k for k in WIDE_FAR} | {-sides(u) * k for k in WIDE_NEAR} for u in range(LANES)
    ]
    spreads = [two_sided(SPREAD_FAR, SPREAD_NEAR, -sides(u)) for u in range(LANES)]
    return sums, wide, spreads


def children(tree, k):
    return sorted((c for c, p in tree.items() if p == k), key=lambda c: -abs(c - k))


def plan(sum_trees, wide, spread_trees):
    kb = 72.0 / LANES
    free = {1: 0.0, -1: 0.0}
    arrive = {}
    clock = 0.0
    order = []

    def send(key, dist, kb, now):
        way = 1 if dist > 0 else -1
        hops = abs(dist)
        begin = max(free[way], now)
        free[way] = begin + kb * 2 * hops / RATE
        arrive[key] = begin + kb * 2 / BURST + FIXED + HOP * hops

    todo = []
    for u in range(LANES):
        todo.append(("mm", u, 0))
        todo += [("sum", u, k) for k in sorted(sum_trees[u], key=lambda k: -abs(k - sum_trees[u][k]))]
        todo.append(("own", u, 0))
        todo += [("spread", u, k) for k in spread_trees[u] if children(spread_trees[u], k)]
        todo.append(("fin", u, 0))
        todo.append(("grad", u, 0))
    done = set()
    cost = {"mm": 0.33, "sum": 0.06, "own": 0.1, "spread": 0.04, "fin": 0.3, "grad": 0.17}
    last = {"mm": 0, "grad": 1e6}

    def ready(task):
        kind, u, k = task
        if kind == "mm":
            return 0.0 if u == 0 or ("mm", u - 1, 0) in done else None
        if kind == "sum" or kind == "own":
            if ("mm", u, 0) not in done:
                return None
            keys = [("sum", u, c) for c in children(sum_trees[u], k)]
        elif kind == "spread":
            keys = [("spread", u, k)]
        elif kind == "fin":
            if ("own", u, 0) not in done:
                return None
            keys = [("spread", u, c) for c in spread_trees[u]]
        else:
            return 0.0 if ("fin", u, 0) in done else None
        if any(key not in arrive for key in keys):
            return None
        return max([0.0] + [arrive[key] for key in keys])

    while todo:
        best = None
        for task in todo:
            at = ready(task)
            if at is None:
                continue
            rank = (max(at, clock) + last.get(task[0], 0.0), task[1], at)
            if best is None or rank < best[0]:
                best = (rank, task, at)
        _, task, at = best
        kind, u, k = task
        clock = max(clock, at) + cost[kind]
        if kind == "sum":
            send(("sum", u, k), k - sum_trees[u][k], kb * (2 if k in wide[u] else 1), clock)
        elif kind in ("own", "spread"):
            for c in children(spread_trees[u], k):
                send(("spread", u, c), c - k, kb, clock)
        order.append(task)
        done.add(task)
        todo.remove(task)
    return order, clock


def offsets(sum_trees, spread_trees):
    found = set()
    for tree in sum_trees:
        found |= {(k - p) % NZ for k, p in tree.items()}
    for tree in spread_trees:
        found |= {(k - p) % NZ for k, p in tree.items()}
    found |= {(-o) % NZ for o in found}
    return sorted(found)


def torus(step):
    return min(step, 4 - step)


STEPS = sorted(
    [(dx, dy) for dx in range(NX) for dy in range(NY) if (dx, dy) != (0, 0)],
    key=lambda s: -(torus(s[0]) + torus(s[1])),
)
COLUMNS = [0, 1, 3, 2]


def dot(a, b, dims):
    return lax.dot_general(a, b, (dims, ((), ())), preferred_element_type=F32)


NN, NT, TN = ((1,), (0,)), ((1,), (1,)), ((0,), (0,))


def kernel(
    sum_trees, wide, spread_trees, order,
    rows, gate_w, up_w, down_w,
    mixed, input_grad, gate_grad, up_grad, down_grad,
    gw, uw, dw, slabs, xs, gs, part, slot, low_out, low_in, acts, halves, sib, dsend, drecv,
    w_sem, a_send, a_recv, f_send, f_recv,
    sum_send, sum_recv, spread_send, spread_recv, h_send, h_recv, d_send, d_recv,
):
    row, z = lax.axis_index("row"), lax.axis_index("col")
    core, chip = row % 2, row // 2
    x, y = chip // NY, chip % NY
    sibling = (chip * 2 + 1 - core, z)

    def plane(dx, dy):
        return ((x + dx) % NX) * NY + (y + dy) % NY

    barrier = pltpu.get_barrier_semaphore()
    around = offsets(sum_trees, spread_trees)
    for dx, dy in STEPS:
        pl.semaphore_signal(
            barrier, inc=1, device_id=(plane(dx, dy) * 2 + core, z), device_id_type=MESH
        )
    for o in around:
        pl.semaphore_signal(barrier, inc=1, device_id=(row, (z + o) % NZ), device_id_type=MESH)
    pl.semaphore_signal(barrier, inc=1, device_id=sibling, device_id_type=MESH)
    loads = [
        pltpu.make_async_copy(src, dst, w_sem.at[i])
        for i, (src, dst) in enumerate(
            ((gate_w, gw), (up_w, uw), (down_w, dw), (rows, slabs.at[core, x, y]))
        )
    ]
    for load in reversed(loads):
        load.start()
    for load in loads[3:]:
        load.wait()
    pl.semaphore_wait(barrier, len(STEPS) + len(around) + 1)

    def gather(dx, dy, from_x, from_y):
        return pltpu.make_async_remote_copy(
            src_ref=slabs.at[core, from_x, from_y],
            dst_ref=slabs.at[core, from_x, from_y],
            send_sem=a_send.at[dx * NY + dy],
            recv_sem=a_recv.at[dx * NY + dy],
            device_id=(plane(dx, dy) * 2 + core, z),
            device_id_type=MESH,
        )

    def forward(dx, which):
        return pltpu.make_async_remote_copy(
            src_ref=slabs.at[which, (x - dx) % NX],
            dst_ref=slabs.at[which, (x - dx) % NX],
            send_sem=f_send.at[dx],
            recv_sem=f_recv.at[dx],
            device_id=sibling,
            device_id_type=MESH,
        )

    for dx, dy in STEPS:
        gather(dx, dy, x, y).start()
    for dx in COLUMNS:
        for dy in range(NY):
            if (dx, dy) in STEPS:
                gather(dx, dy, (x - dx) % NX, (y - dy) % NY).wait_recv()
        forward(dx, core).start()
    def unpack(which):
        rows, place = slabs[which].astype(F32), pl.ds(which * 128, 128)
        xs[place, :] = rows[:, :, 0:8, :].reshape(128, 512).astype(BF16)
        gs[place, :] = rows[:, :, 8:16, :].reshape(128, 512).astype(BF16)

    unpack(core)
    for load in loads[:3]:
        load.wait()
    for dx in COLUMNS:
        forward(dx, 1 - core).wait_recv()
    unpack(1 - core)

    def index(tree, k):
        return sorted(tree).index(k)

    def sum_copy(u, k):
        o = k - sum_trees[u][k]
        i = index(sum_trees[u], k)
        return pltpu.make_async_remote_copy(
            src_ref=part.at[u, (z + k) % NZ] if k in wide[u] else low_out.at[u, i],
            dst_ref=slot.at[u, i] if k in wide[u] else low_in.at[u, i],
            send_sem=sum_send.at[u, i],
            recv_sem=sum_recv.at[u, i],
            device_id=(row, (z + o) % NZ),
            device_id_type=MESH,
        )

    def spread_copy(u, c, chunk):
        o = c - spread_trees[u][c]
        i = index(spread_trees[u], c)
        return pltpu.make_async_remote_copy(
            src_ref=acts.at[u, chunk],
            dst_ref=acts.at[u, chunk],
            send_sem=spread_send.at[u, i],
            recv_sem=spread_recv.at[u, i],
            device_id=(row, (z + o) % NZ),
            device_id_type=MESH,
        )

    def gathered(u, k, total):
        for c in children(sum_trees[u], k):
            sum_copy(u, c).wait_recv()
            i = index(sum_trees[u], c)
            total += slot[u, i] if c in wide[u] else low_in[u, i].astype(F32)
        return total

    def spread_wait(u, k):
        spread_copy(u, k, (z - k) % NZ).wait_recv()

    begun = False
    for kind, u, k in order:
        unit = pl.ds(u * W, W)
        if kind == "mm":
            part[u, :, :, 0:W] = dot(xs[...], gw[:, unit], NN).reshape(NZ, 16, W)
            part[u, :, :, W : 2 * W] = dot(xs[...], uw[:, unit], NN).reshape(NZ, 16, W)
            part[u, :, :, 2 * W : 3 * W] = dot(gs[...], dw[unit, :], NT).reshape(NZ, 16, W)
        elif kind == "sum":
            chunk = (z + k) % NZ
            total = gathered(u, k, part[u, chunk])
            if k not in wide[u]:
                low_out[u, index(sum_trees[u], k)] = total.astype(BF16)
            elif children(sum_trees[u], k):
                part[u, chunk] = total
            sum_copy(u, k).start()
        elif kind == "own":
            total = gathered(u, 0, part[u, z])
            gate, up, hidden_grad = total[:, 0:W], total[:, W : 2 * W], total[:, 2 * W :]
            sig = jax.nn.sigmoid(gate)
            swish = gate * sig
            acts[u, z, :, 0:W] = (swish * up).astype(BF16)
            acts[u, z, :, W : 2 * W] = (
                hidden_grad * up * sig * (1.0 + gate * (1.0 - sig))
            ).astype(BF16)
            acts[u, z, :, 2 * W : 3 * W] = (hidden_grad * swish).astype(BF16)
            for c in children(spread_trees[u], 0):
                spread_copy(u, c, z).start()
        elif kind == "spread":
            spread_wait(u, k)
            for c in children(spread_trees[u], k):
                spread_copy(u, c, (z - k) % NZ).start()
        elif kind == "fin":
            for c in spread_trees[u]:
                if not children(spread_trees[u], c):
                    spread_wait(u, c)
            hidden = acts[u, :, :, 0:W].reshape(256, W)
            gate_delta = acts[u, :, :, W : 2 * W].reshape(256, W)
            up_delta = acts[u, :, :, 2 * W : 3 * W].reshape(256, W)
            out = dot(hidden, dw[unit, :], NN).reshape(2, 16, 8, 512)
            back = (dot(gate_delta, gw[:, unit], NT) + dot(up_delta, uw[:, unit], NT)).reshape(
                2, 16, 8, 512
            )
            if begun:
                out += halves[:, :, 0:8, :]
                back += halves[:, :, 8:16, :]
            halves[:, :, 0:8, :] = out
            halves[:, :, 8:16, :] = back
            begun = True
        else:
            hidden = acts[u, :, :, 0:W].reshape(256, W)
            gate_delta = acts[u, :, :, W : 2 * W].reshape(256, W)
            up_delta = acts[u, :, :, 2 * W : 3 * W].reshape(256, W)
            gate_grad[:, unit] = dot(xs[...], gate_delta, TN).astype(BF16)
            up_grad[:, unit] = dot(xs[...], up_delta, TN).astype(BF16)
            down_grad[unit, :] = dot(hidden, gs[...], TN).astype(BF16)
        if kind == "fin" and (kind, u, k) == [t for t in order if t[0] == "fin"][-1]:
            def half(dx):
                chips = pl.ds((x + dx) % NX * NY, NY)
                return pltpu.make_async_remote_copy(
                    src_ref=halves.at[1 - core, chips],
                    dst_ref=sib.at[chips],
                    send_sem=h_send.at[dx],
                    recv_sem=h_recv.at[dx],
                    device_id=sibling,
                    device_id_type=MESH,
                )

            for dx in reversed(COLUMNS):
                half(dx).start()

            def scatter(dx, dy):
                return pltpu.make_async_remote_copy(
                    src_ref=dsend.at[plane(dx, dy)],
                    dst_ref=drecv.at[dx * NY + dy],
                    send_sem=d_send.at[dx * NY + dy],
                    recv_sem=d_recv.at[dx * NY + dy],
                    device_id=(plane(dx, dy) * 2 + core, z),
                    device_id_type=MESH,
                )

            for dx in reversed(COLUMNS):
                half(dx).wait_recv()
                for dy in (2, 1, 3, 0):
                    if (dx, dy) in STEPS:
                        to = plane(dx, dy)
                        dsend[to] = (halves[core, to] + sib[to]).astype(BF16)
                        scatter(dx, dy).start()

    for dx, dy in STEPS:
        gather(dx, dy, x, y).wait_send()
    for dx in COLUMNS:
        forward(dx, core).wait_send()
    for u in range(LANES):
        for k in sum_trees[u]:
            sum_copy(u, k).wait_send()
        for k in spread_trees[u]:
            spread_copy(u, k, z).wait_send()
    for dx in COLUMNS:
        half(dx).wait_send()
    total = halves[core, chip] + sib[chip]
    for dx, dy in reversed(STEPS):
        scatter(dx, dy).wait_recv()
        total += drecv[dx * NY + dy].astype(F32)
    mixed[...] = total[0:8].astype(BF16)
    input_grad[...] = total[8:16].astype(BF16)
    for dx, dy in STEPS:
        scatter(dx, dy).wait_send()


def hand_on(*refs):
    copies = [pltpu.make_async_copy(refs[i], refs[5 + i], refs[10].at[i]) for i in range(5)]
    for copy in copies:
        copy.start()
    for copy in copies:
        copy.wait()


def shards(tokens, gate_weight, up_weight, down_weight, out_grad):
    sum_trees, wide, spread_trees = trees()
    order, _ = plan(sum_trees, wide, spread_trees)
    anywhere = pl.BlockSpec(memory_space=pl.ANY)
    dma = pltpu.SemaphoreType.DMA
    shape = jax.ShapeDtypeStruct
    outs = pl.pallas_call(
        functools.partial(kernel, sum_trees, wide, spread_trees, order),
        out_shape=(
            shape((8, 512), BF16),
            shape((8, 512), BF16),
            shape((512, 768), BF16),
            shape((512, 768), BF16),
            shape((768, 512), BF16),
        ),
        in_specs=[anywhere] * 4,
        out_specs=(pl.BlockSpec(memory_space=pltpu.VMEM),) * 5,
        scratch_shapes=[
            pltpu.VMEM((512, 768), BF16),
            pltpu.VMEM((512, 768), BF16),
            pltpu.VMEM((768, 512), BF16),
            pltpu.VMEM((2, NX, NY, 16, 512), BF16),
            pltpu.VMEM((256, 512), BF16),
            pltpu.VMEM((256, 512), BF16),
            pltpu.VMEM((LANES, NZ, 16, 3 * W), F32),
            pltpu.VMEM((LANES, NZ - 1, 16, 3 * W), F32),
            pltpu.VMEM((LANES, NZ - 1, 16, 3 * W), BF16),
            pltpu.VMEM((LANES, NZ - 1, 16, 3 * W), BF16),
            pltpu.VMEM((LANES, NZ, 16, 3 * W), BF16),
            pltpu.VMEM((2, 16, 16, 512), F32),
            pltpu.VMEM((16, 16, 512), F32),
            pltpu.VMEM((16, 16, 512), BF16),
            pltpu.VMEM((16, 16, 512), BF16),
            dma((5,)),
            dma((16,)), dma((16,)), dma((4,)), dma((4,)),
            dma((LANES, NZ - 1)), dma((LANES, NZ - 1)),
            dma((LANES, NZ - 1)), dma((LANES, NZ - 1)),
            dma((4,)), dma((4,)), dma((16,)), dma((16,)),
        ],
        compiler_params=pltpu.CompilerParams(
            collective_id=0, has_side_effects=True, vmem_limit_bytes=205 * 2**18
        ),
    )(jnp.concatenate([tokens, out_grad], axis=0), gate_weight, up_weight, down_weight)
    return pl.pallas_call(
        hand_on,
        out_shape=tuple(shape(o.shape, o.dtype) for o in outs),
        in_specs=[pl.BlockSpec(memory_space=pltpu.VMEM)] * 5,
        out_specs=(anywhere,) * 5,
        scratch_shapes=[dma((5,))],
        compiler_params=pltpu.CompilerParams(vmem_limit_bytes=4 * 2**20),
    )(*outs)


def solution(mesh):
    return jax.shard_map(
        shards,
        mesh=mesh,
        in_specs=(
            P("row", "col"),
            P("col", "row"),
            P("col", "row"),
            P("row", "col"),
            P("row", "col"),
        ),
        out_specs=(
            P("row", "col"),
            P("row", "col"),
            P("col", "row"),
            P("col", "row"),
            P("row", "col"),
        ),
        check_vma=False,
    )
```

```python
import functools

import jax
import jax.numpy as jnp
from jax import lax
from jax.experimental import pallas as pl
from jax.experimental.pallas import tpu as pltpu
from jax.sharding import PartitionSpec as P

MESH = pl.DeviceIdType.MESH
F32, BF16 = jnp.float32, jnp.bfloat16
NZ, NX, NY = 16, 4, 4
LANES, W = 3, 256

SUM_FAR = {1: 0, 2: 1, 3: 2, 4: 3, 5: 6, 6: 3, 7: 6, 8: 6}
SUM_NEAR = {1: 0, 2: 1, 3: 2, 4: 5, 5: 2, 6: 5, 7: 5}
WIDE_FAR, WIDE_NEAR = (1, 2, 3), (1, 2)
SPREAD_FAR = {1: 0, 2: 0, 3: 2, 4: 2, 5: 4, 6: 4, 7: 6, 8: 6}
SPREAD_NEAR = {1: 0, 2: 0, 3: 2, 4: 2, 5: 4, 6: 4, 7: 6}
RATE, BURST, FIXED, HOP = 95.0, 130.0, 2.35, 0.65


def two_sided(far, near, way):
    return {**{way * k: way * p for k, p in far.items()}, **{-way * k: -way * p for k, p in near.items()}}


def sides(u):
    return 1 if u % 2 == 0 else -1


def trees():
    sums = [two_sided(SUM_FAR, SUM_NEAR, sides(u)) for u in range(LANES)]
    wide = [
        {sides(u) * k for k in WIDE_FAR} | {-sides(u) * k for k in WIDE_NEAR} for u in range(LANES)
    ]
    spreads = [two_sided(SPREAD_FAR, SPREAD_NEAR, -sides(u)) for u in range(LANES)]
    return sums, wide, spreads


def children(tree, k):
    return sorted((c for c, p in tree.items() if p == k), key=lambda c: -abs(c - k))


def plan(sum_trees, wide, spread_trees):
    kb = 72.0 / LANES
    free = {1: 0.0, -1: 0.0}
    arrive = {}
    clock = 0.0
    order = []

    def send(key, dist, kb, now):
        way = 1 if dist > 0 else -1
        hops = abs(dist)
        begin = max(free[way], now)
        free[way] = begin + kb * 2 * hops / RATE
        arrive[key] = begin + kb * 2 / BURST + FIXED + HOP * hops

    todo = []
    for u in range(LANES):
        todo.append(("mm", u, 0))
        todo += [("sum", u, k) for k in sorted(sum_trees[u], key=lambda k: -abs(k - sum_trees[u][k]))]
        todo.append(("own", u, 0))
        todo += [("spread", u, k) for k in spread_trees[u] if children(spread_trees[u], k)]
        todo.append(("fin", u, 0))
        todo.append(("grad", u, 0))
    done = set()
    cost = {"mm": 0.33, "sum": 0.06, "own": 0.1, "spread": 0.04, "fin": 0.3, "grad": 0.17}
    last = {"mm": 0, "grad": 1e6}

    def ready(task):
        kind, u, k = task
        if kind == "mm":
            return 0.0 if u == 0 or ("mm", u - 1, 0) in done else None
        if kind == "sum" or kind == "own":
            if ("mm", u, 0) not in done:
                return None
            keys = [("sum", u, c) for c in children(sum_trees[u], k)]
        elif kind == "spread":
            keys = [("spread", u, k)]
        elif kind == "fin":
            if ("own", u, 0) not in done:
                return None
            keys = [("spread", u, c) for c in spread_trees[u]]
        else:
            return 0.0 if ("fin", u, 0) in done else None
        if any(key not in arrive for key in keys):
            return None
        return max([0.0] + [arrive[key] for key in keys])

    while todo:
        best = None
        for task in todo:
            at = ready(task)
            if at is None:
                continue
            rank = (max(at, clock) + last.get(task[0], 0.0), task[1], at)
            if best is None or rank < best[0]:
                best = (rank, task, at)
        _, task, at = best
        kind, u, k = task
        clock = max(clock, at) + cost[kind]
        if kind == "sum":
            send(("sum", u, k), k - sum_trees[u][k], kb * (2 if k in wide[u] else 1), clock)
        elif kind in ("own", "spread"):
            for c in children(spread_trees[u], k):
                send(("spread", u, c), c - k, kb, clock)
        order.append(task)
        done.add(task)
        todo.remove(task)
    return order, clock


def offsets(sum_trees, spread_trees):
    found = set()
    for tree in sum_trees:
        found |= {(k - p) % NZ for k, p in tree.items()}
    for tree in spread_trees:
        found |= {(k - p) % NZ for k, p in tree.items()}
    found |= {(-o) % NZ for o in found}
    return sorted(found)


def torus(step):
    return min(step, 4 - step)


STEPS = sorted(
    [(dx, dy) for dx in range(NX) for dy in range(NY) if (dx, dy) != (0, 0)],
    key=lambda s: -(torus(s[0]) + torus(s[1])),
)
COLUMNS = [0, 1, 3, 2]


def dot(a, b, dims):
    return lax.dot_general(a, b, (dims, ((), ())), preferred_element_type=F32)


NN, NT, TN = ((1,), (0,)), ((1,), (1,)), ((0,), (0,))


def kernel(
    sum_trees, wide, spread_trees, order,
    rows, gate_w, up_w, down_w,
    mixed, input_grad, gate_grad, up_grad, down_grad,
    gw, uw, dw, slabs, xs, gs, part, slot, low_out, low_in, acts, halves, sib, dsend, drecv,
    w_sem, a_send, a_recv, f_send, f_recv,
    sum_send, sum_recv, spread_send, spread_recv, h_send, h_recv, d_send, d_recv,
):
    row, z = lax.axis_index("row"), lax.axis_index("col")
    core, chip = row % 2, row // 2
    x, y = chip // NY, chip % NY
    sibling = (chip * 2 + 1 - core, z)

    def plane(dx, dy):
        return ((x + dx) % NX) * NY + (y + dy) % NY

    barrier = pltpu.get_barrier_semaphore()
    around = offsets(sum_trees, spread_trees)
    for dx, dy in STEPS:
        pl.semaphore_signal(
            barrier, inc=1, device_id=(plane(dx, dy) * 2 + core, z), device_id_type=MESH
        )
    for o in around:
        pl.semaphore_signal(barrier, inc=1, device_id=(row, (z + o) % NZ), device_id_type=MESH)
    pl.semaphore_signal(barrier, inc=1, device_id=sibling, device_id_type=MESH)
    loads = [
        pltpu.make_async_copy(src, dst, w_sem.at[i])
        for i, (src, dst) in enumerate(
            ((gate_w, gw), (up_w, uw), (down_w, dw), (rows, slabs.at[core, x, y]))
        )
    ]
    for load in reversed(loads):
        load.start()
    for load in loads[3:]:
        load.wait()
    pl.semaphore_wait(barrier, len(STEPS) + len(around) + 1)

    def gather(dx, dy, from_x, from_y):
        return pltpu.make_async_remote_copy(
            src_ref=slabs.at[core, from_x, from_y],
            dst_ref=slabs.at[core, from_x, from_y],
            send_sem=a_send.at[dx * NY + dy],
            recv_sem=a_recv.at[dx * NY + dy],
            device_id=(plane(dx, dy) * 2 + core, z),
            device_id_type=MESH,
        )

    def forward(dx, which):
        return pltpu.make_async_remote_copy(
            src_ref=slabs.at[which, (x - dx) % NX],
            dst_ref=slabs.at[which, (x - dx) % NX],
            send_sem=f_send.at[dx],
            recv_sem=f_recv.at[dx],
            device_id=sibling,
            device_id_type=MESH,
        )

    for dx, dy in STEPS:
        gather(dx, dy, x, y).start()
    for dx in COLUMNS:
        for dy in range(NY):
            if (dx, dy) in STEPS:
                gather(dx, dy, (x - dx) % NX, (y - dy) % NY).wait_recv()
        forward(dx, core).start()
    def unpack(which):
        rows, place = slabs[which].astype(F32), pl.ds(which * 128, 128)
        xs[place, :] = rows[:, :, 0:8, :].reshape(128, 512).astype(BF16)
        gs[place, :] = rows[:, :, 8:16, :].reshape(128, 512).astype(BF16)

    unpack(core)
    for load in loads[:3]:
        load.wait()
    for dx in COLUMNS:
        forward(dx, 1 - core).wait_recv()
    unpack(1 - core)

    def index(tree, k):
        return sorted(tree).index(k)

    def sum_copy(u, k):
        o = k - sum_trees[u][k]
        i = index(sum_trees[u], k)
        return pltpu.make_async_remote_copy(
            src_ref=part.at[u, (z + k) % NZ] if k in wide[u] else low_out.at[u, i],
            dst_ref=slot.at[u, i] if k in wide[u] else low_in.at[u, i],
            send_sem=sum_send.at[u, i],
            recv_sem=sum_recv.at[u, i],
            device_id=(row, (z + o) % NZ),
            device_id_type=MESH,
        )

    def spread_copy(u, c, chunk):
        o = c - spread_trees[u][c]
        i = index(spread_trees[u], c)
        return pltpu.make_async_remote_copy(
            src_ref=acts.at[u, chunk],
            dst_ref=acts.at[u, chunk],
            send_sem=spread_send.at[u, i],
            recv_sem=spread_recv.at[u, i],
            device_id=(row, (z + o) % NZ),
            device_id_type=MESH,
        )

    def gathered(u, k, total):
        for c in children(sum_trees[u], k):
            sum_copy(u, c).wait_recv()
            i = index(sum_trees[u], c)
            total += slot[u, i] if c in wide[u] else low_in[u, i].astype(F32)
        return total

    def spread_wait(u, k):
        spread_copy(u, k, (z - k) % NZ).wait_recv()

    begun = False
    for kind, u, k in order:
        unit = pl.ds(u * W, W)
        if kind == "mm":
            part[u, :, :, 0:W] = dot(xs[...], gw[:, unit], NN).reshape(NZ, 16, W)
            part[u, :, :, W : 2 * W] = dot(xs[...], uw[:, unit], NN).reshape(NZ, 16, W)
            part[u, :, :, 2 * W : 3 * W] = dot(gs[...], dw[unit, :], NT).reshape(NZ, 16, W)
        elif kind == "sum":
            chunk = (z + k) % NZ
            total = gathered(u, k, part[u, chunk])
            if k not in wide[u]:
                low_out[u, index(sum_trees[u], k)] = total.astype(BF16)
            elif children(sum_trees[u], k):
                part[u, chunk] = total
            sum_copy(u, k).start()
        elif kind == "own":
            total = gathered(u, 0, part[u, z])
            gate, up, hidden_grad = total[:, 0:W], total[:, W : 2 * W], total[:, 2 * W :]
            sig = jax.nn.sigmoid(gate)
            swish = gate * sig
            acts[u, z, :, 0:W] = (swish * up).astype(BF16)
            acts[u, z, :, W : 2 * W] = (
                hidden_grad * up * sig * (1.0 + gate * (1.0 - sig))
            ).astype(BF16)
            acts[u, z, :, 2 * W : 3 * W] = (hidden_grad * swish).astype(BF16)
            for c in children(spread_trees[u], 0):
                spread_copy(u, c, z).start()
        elif kind == "spread":
            spread_wait(u, k)
            for c in children(spread_trees[u], k):
                spread_copy(u, c, (z - k) % NZ).start()
        elif kind == "fin":
            for c in spread_trees[u]:
                if not children(spread_trees[u], c):
                    spread_wait(u, c)
            hidden = acts[u, :, :, 0:W].reshape(256, W)
            gate_delta = acts[u, :, :, W : 2 * W].reshape(256, W)
            up_delta = acts[u, :, :, 2 * W : 3 * W].reshape(256, W)
            out = dot(hidden, dw[unit, :], NN).reshape(2, 16, 8, 512)
            back = (dot(gate_delta, gw[:, unit], NT) + dot(up_delta, uw[:, unit], NT)).reshape(
                2, 16, 8, 512
            )
            if begun:
                out += halves[:, :, 0:8, :]
                back += halves[:, :, 8:16, :]
            halves[:, :, 0:8, :] = out
            halves[:, :, 8:16, :] = back
            begun = True
        else:
            hidden = acts[u, :, :, 0:W].reshape(256, W)
            gate_delta = acts[u, :, :, W : 2 * W].reshape(256, W)
            up_delta = acts[u, :, :, 2 * W : 3 * W].reshape(256, W)
            gate_grad[:, unit] = dot(xs[...], gate_delta, TN).astype(BF16)
            up_grad[:, unit] = dot(xs[...], up_delta, TN).astype(BF16)
            down_grad[unit, :] = dot(hidden, gs[...], TN).astype(BF16)
        if kind == "fin" and (kind, u, k) == [t for t in order if t[0] == "fin"][-1]:
            def half(dx):
                chips = pl.ds((x + dx) % NX * NY, NY)
                return pltpu.make_async_remote_copy(
                    src_ref=halves.at[1 - core, chips],
                    dst_ref=sib.at[chips],
                    send_sem=h_send.at[dx],
                    recv_sem=h_recv.at[dx],
                    device_id=sibling,
                    device_id_type=MESH,
                )

            for dx in reversed(COLUMNS):
                half(dx).start()

            def scatter(dx, dy):
                return pltpu.make_async_remote_copy(
                    src_ref=dsend.at[plane(dx, dy)],
                    dst_ref=drecv.at[dx * NY + dy],
                    send_sem=d_send.at[dx * NY + dy],
                    recv_sem=d_recv.at[dx * NY + dy],
                    device_id=(plane(dx, dy) * 2 + core, z),
                    device_id_type=MESH,
                )

            for dx in reversed(COLUMNS):
                half(dx).wait_recv()
                for dy in (2, 1, 3, 0):
                    if (dx, dy) in STEPS:
                        to = plane(dx, dy)
                        dsend[to] = (halves[core, to] + sib[to]).astype(BF16)
                        scatter(dx, dy).start()

    for dx, dy in STEPS:
        gather(dx, dy, x, y).wait_send()
    for dx in COLUMNS:
        forward(dx, core).wait_send()
    for u in range(LANES):
        for k in sum_trees[u]:
            sum_copy(u, k).wait_send()
        for k in spread_trees[u]:
            spread_copy(u, k, z).wait_send()
    for dx in COLUMNS:
        half(dx).wait_send()
    total = halves[core, chip] + sib[chip]
    for dx, dy in reversed(STEPS):
        scatter(dx, dy).wait_recv()
        total += drecv[dx * NY + dy].astype(F32)
    mixed[...] = total[0:8].astype(BF16)
    input_grad[...] = total[8:16].astype(BF16)
    for dx, dy in STEPS:
        scatter(dx, dy).wait_send()


def hand_on(*refs):
    copies = [pltpu.make_async_copy(refs[i], refs[5 + i], refs[10].at[i]) for i in range(5)]
    for copy in copies:
        copy.start()
    for copy in copies:
        copy.wait()


def shards(tokens, gate_weight, up_weight, down_weight, out_grad):
    sum_trees, wide, spread_trees = trees()
    order, _ = plan(sum_trees, wide, spread_trees)
    anywhere = pl.BlockSpec(memory_space=pl.ANY)
    dma = pltpu.SemaphoreType.DMA
    shape = jax.ShapeDtypeStruct
    outs = pl.pallas_call(
        functools.partial(kernel, sum_trees, wide, spread_trees, order),
        out_shape=(
            shape((8, 512), BF16),
            shape((8, 512), BF16),
            shape((512, 768), BF16),
            shape((512, 768), BF16),
            shape((768, 512), BF16),
        ),
        in_specs=[anywhere] * 4,
        out_specs=(pl.BlockSpec(memory_space=pltpu.VMEM),) * 5,
        scratch_shapes=[
            pltpu.VMEM((512, 768), BF16),
            pltpu.VMEM((512, 768), BF16),
            pltpu.VMEM((768, 512), BF16),
            pltpu.VMEM((2, NX, NY, 16, 512), BF16),
            pltpu.VMEM((256, 512), BF16),
            pltpu.VMEM((256, 512), BF16),
            pltpu.VMEM((LANES, NZ, 16, 3 * W), F32),
            pltpu.VMEM((LANES, NZ - 1, 16, 3 * W), F32),
            pltpu.VMEM((LANES, NZ - 1, 16, 3 * W), BF16),
            pltpu.VMEM((LANES, NZ - 1, 16, 3 * W), BF16),
            pltpu.VMEM((LANES, NZ, 16, 3 * W), BF16),
            pltpu.VMEM((2, 16, 16, 512), F32),
            pltpu.VMEM((16, 16, 512), F32),
            pltpu.VMEM((16, 16, 512), BF16),
            pltpu.VMEM((16, 16, 512), BF16),
            dma((5,)),
            dma((16,)), dma((16,)), dma((4,)), dma((4,)),
            dma((LANES, NZ - 1)), dma((LANES, NZ - 1)),
            dma((LANES, NZ - 1)), dma((LANES, NZ - 1)),
            dma((4,)), dma((4,)), dma((16,)), dma((16,)),
        ],
        compiler_params=pltpu.CompilerParams(
            collective_id=0, has_side_effects=True, vmem_limit_bytes=205 * 2**18
        ),
    )(jnp.concatenate([tokens, out_grad], axis=0), gate_weight, up_weight, down_weight)
    return pl.pallas_call(
        hand_on,
        out_shape=tuple(shape(o.shape, o.dtype) for o in outs),
        in_specs=[pl.BlockSpec(memory_space=pltpu.VMEM)] * 5,
        out_specs=(anywhere,) * 5,
        scratch_shapes=[dma((5,))],
        compiler_params=pltpu.CompilerParams(vmem_limit_bytes=4 * 2**20),
    )(*outs)


def solution(mesh):
    return jax.shard_map(
        shards,
        mesh=mesh,
        in_specs=(
            P("row", "col"),
            P("col", "row"),
            P("col", "row"),
            P("row", "col"),
            P("row", "col"),
        ),
        out_specs=(
            P("row", "col"),
            P("row", "col"),
            P("col", "row"),
            P("col", "row"),
            P("row", "col"),
        ),
        check_vma=False,
    )
```
